256 devices in a mesh: dp: 2 (over core), expert: 128 (over z, y, x).
Axes of the slice: x: 4, y: 4, z: 8, core: 2. Of those that a mesh axis runs over, the one named last changes fastest.
Arguments:
- queries: bfloat16 [32768, 5120], P(('dp', 'expert')), may hold values from -6 to 6
- key_rows: bfloat16 [32768, 1024], P(('dp', 'expert')), may hold values from -6 to 6
- value_rows: bfloat16 [32768, 1024], P(('dp', 'expert')), may hold values from -6 to 6
- segments: int32 [256, 128], P(('dp', 'expert')), may hold values from 0 to 3, never falling along the last dimension, each value on 1 to 64 neighbouring positions
- swap_flags: int32 [128], P('expert'), may hold values 0 or 1
- expert_ids: int32 [32768, 1], P(('dp', 'expert')), may hold values from 0 to 15; in each aligned block of 128 rows (0 to 127, 128 to 255, ...) at most 10 rows name the same one
- norm_gain: bfloat16 [5120], replicated, may hold values from 0.25 to 1.75
- gate_weight: bfloat16 [5120, 32768], P(None, 'expert'), may hold values from -0.078125 to 0.078125
- up_weight: bfloat16 [5120, 32768], P(None, 'expert'), may hold values from -0.078125 to 0.078125
- down_weight: bfloat16 [32768, 5120], P('expert'), may hold values from -0.0625 to 0.0625
Outputs:
- layer_out: bfloat16 [32768, 5120], P(('dp', 'expert'))
The draws below stay inside these ranges and needn't reach their ends.
Inputs may be any that keep to these rules, and one draw needn't show every extreme that they name: `expert_ids`: within each pack, no expert id is named by more than 10 tokens, and some ids are named by exactly 10 tokens in some packs. `segments`: within each pack the document number never falls.
All inputs are finite; a program needn't handle non-finite values. No bound on the sum of `swap_flags` on one device may be relied on, other than what follows from the above.
Results may differ from the reference program's by a relative error of at most 0.015.
Values may be sent and summed in bfloat16 or wider, within the bound.
No kernel may reach another device: no remote copies, remote signals or barrier semaphores. Data moves between devices by JAX's collectives and lax.ppermute only.
A program may use at most 192 MiB of HBM per device.

```python
import math
import jax
import jax.numpy as jnp
import numpy as np
from jax import lax

D = 5120
HEADS = 40
KVH = 8
HD = 128
FFW = 8192
ROUTES = 16
EXP_WIN = 4
CAP = 10
TOK_DEV = 128
SHARDS = 32
FF_DEV = 256
PACKS = 256
TOKENS = 32768
N_DP = 2
N_EXPERT = 128


def draw_queries(key, part):
    key = jax.random.fold_in(key, 5)
    result = jnp.clip(jax.random.normal(key, (TOKENS, HEADS * HD), jnp.float32), -6.0, 6.0)
    return result.astype(jnp.bfloat16)


def draw_key_rows(key, part):
    key = jax.random.fold_in(key, 9)
    result = jnp.clip(jax.random.normal(key, (TOKENS, KVH * HD), jnp.float32), -6.0, 6.0)
    return result.astype(jnp.bfloat16)


def plant(values, stream_key, low, high):
    index_at = [jax.random.randint(jax.random.fold_in(stream_key, axis), (), 0, length) for axis, length in enumerate(values.shape)]
    widest = values.shape.index(max(values.shape))
    beside = index_at[:widest] + [(index_at[widest] + 1) % values.shape[widest]] + index_at[widest + 1:]
    return values.at[tuple(index_at)].set(low).at[tuple(beside)].set(high)


def block_levels(stream_key, shape, shards, least, high):
    def one(axis_at, parts):
        heights = jax.random.uniform(jax.random.fold_in(jax.random.fold_in(stream_key, 6), axis_at), (parts,), jnp.float32, least / len(shards), high / len(shards))
        return jnp.repeat(jnp.exp(heights), shape[axis_at] // parts).reshape((-1,) + (1,) * (len(shape) - axis_at - 1))

    level = one(*shards[0])
    for cut in shards[1:]:
        level = level * one(*cut)
    return level


def split_up(number_of, total, reach, skew):
    loads = [(1 << 20) // math.isqrt(grade ** skew) + 1 for grade in range(2, number_of + 1)]
    rest, counts = total - reach - (number_of - 1), [1] * (number_of - 1)
    while rest > 0:
        free = [i for i in range(number_of - 1) if counts[i] < reach]
        mass, left = sum([loads[i] for i in free]), rest
        for i in free:
            more = min(reach - counts[i], max(1, left * loads[i] // mass), rest)
            counts[i] = counts[i] + more
            rest = rest - more
    return np.array([reach] + counts)


def ragged_sizes(own_key, count, total, bound, skew):
    if count == 2:
        one = jax.random.randint(own_key, (), max(1, total - bound), min(bound, total - 1) + 1)
        return jnp.stack([one, total - one])
    sizes = jnp.asarray(split_up(count, total, bound, skew), jnp.int32)
    couples = (count - 1) // 2
    giver, taker = sizes[1:1 + 2 * couples:2], sizes[2:2 + 2 * couples:2]
    margin = jnp.minimum(giver - 1, bound - taker)
    passed = jax.random.randint(jax.random.fold_in(own_key, 1), (couples,), 0, 1 << 20) % (margin + 1)
    sizes = sizes.at[1:1 + 2 * couples:2].set(giver - passed).at[2:2 + 2 * couples:2].set(taker + passed)
    return sizes[jax.random.permutation(jax.random.fold_in(own_key, 2), count)]


def deal_out(rng, own, number, rows, count, top, reach, lean):
    sequence = jax.random.permutation(rng, count)
    heavy_load, ordinary = shares(count, rows * top, reach, lean, True), shares(count, rows * top, reach, lean, False)
    places = jnp.arange(count)

    def named(tallies, offset_by):
        used = int((tallies > 0).sum())
        fixed = max(1, used // 4)
        passed = fixed + (places - fixed + offset_by * (used - fixed)) % max(1, count - fixed)
        return jnp.zeros((count,), jnp.int32).at[sequence[jnp.where(places < fixed, places, passed)]].set(jnp.asarray(tallies, jnp.int32))

    tallies = jnp.where(number % 4 == 0, named(heavy_load, number // 4), named(ordinary, number - number // 4 - 1))
    mixed = jax.random.permutation(jax.random.fold_in(own, 3), count)
    source_of, taker = mixed[0:count // 2 * 2:2], mixed[1:count // 2 * 2:2]
    margin = jnp.minimum(tallies[source_of] - 1, reach - tallies[taker]) // 2
    margin = jnp.where((source_of == sequence[0]) | (taker == sequence[0]) | (tallies[taker] == 0), 0, jnp.maximum(margin, 0))
    passed = jax.random.randint(jax.random.fold_in(own, 4), (count // 2,), 0, 1 << 20) % (margin + 1)
    tallies = tallies.at[source_of].add(-passed).at[taker].add(passed)
    labels = jnp.searchsorted(jnp.cumsum(tallies), jnp.arange(rows * top), side="right").astype(jnp.int32)
    grid = labels.reshape(top, rows).T
    grid = grid[jax.random.permutation(jax.random.fold_in(own, 1), rows)]
    offset_by = jax.random.randint(jax.random.fold_in(own, 2), (rows, 1), 0, top)
    return jnp.take_along_axis(grid, (jnp.arange(top)[None, :] + offset_by) % top, axis=1)


def shares(number_of, total, most, skew, full):
    weights = [(1 << 20) // math.isqrt(grade ** skew) + 1 for grade in range(1, number_of + 1)]
    largest = most if full else min(most, max(-(-total // number_of), total * weights[0] // sum(weights)))
    least = 1 if total - largest >= number_of - 1 else 0
    holding, rest = [largest] + [least] * (number_of - 1), total - largest - least * (number_of - 1)
    while rest > 0:
        candidates = [i for i in range(1, number_of) if holding[i] < largest] or [i for i in range(1, number_of) if holding[i] < most]
        mass, remaining = sum([weights[i] for i in candidates]), rest
        for i in candidates:
            more = min(most - holding[i], max(1, remaining * weights[i] // mass), rest)
            holding[i] = holding[i] + more
            rest = rest - more
    return np.array(holding)


def gaussian(key, shape, deviation, bound, cuts=(), kind=jnp.bfloat16):
    entries = jax.random.normal(key, shape, jnp.float32) * deviation
    if len(cuts) > 0:
        entries = block_levels(key, shape, cuts, -0.22, 0.18) * entries
    return jnp.clip(entries, min=-bound, max=bound).astype(kind)


def setup_inputs(seed: int = 0) -> dict:
    arg_keys = jax.random.split(jax.random.key(seed), 11)
    queries = draw_queries(jax.random.fold_in(arg_keys[10], 71), 0)
    key_rows = draw_key_rows(jax.random.fold_in(arg_keys[10], 71), 0)
    value_rows = gaussian(arg_keys[2], (TOKENS, KVH * HD), 1.0, 6.0, ((0, 256),))
    segments = jax.vmap(lambda own: jnp.searchsorted(jnp.cumsum(ragged_sizes(own, 4, TOK_DEV, TOK_DEV // 2, 2)), jnp.arange(TOK_DEV), side="right"))(jax.random.split(arg_keys[3], PACKS)).reshape((PACKS, TOK_DEV)).astype(jnp.int32)
    swap_flags = plant((jax.random.randint(arg_keys[4], (N_EXPERT,), 0, 2) < 1).astype(jnp.int32), jax.random.fold_in(arg_keys[4], 1), 0, 1)
    expert_ids_keys = jax.random.split(jax.random.fold_in(arg_keys[5], 1), TOKENS // TOK_DEV)
    expert_ids_turns = jax.random.permutation(jax.random.fold_in(arg_keys[5], 3), TOKENS // TOK_DEV)
    expert_ids = jax.vmap(lambda own, number: deal_out(jax.random.fold_in(arg_keys[5], 2), own, number, TOK_DEV, ROUTES, 1, CAP, 2))(expert_ids_keys, expert_ids_turns).reshape((TOKENS, 1))
    norm_gain = jnp.clip(1.0 + 0.15 * jax.random.normal(arg_keys[6], (D,), jnp.float32), 0.25, 1.75).astype(jnp.bfloat16)
    gate_weight = gaussian(arg_keys[7], (D, EXP_WIN * FFW), D ** -0.5, 0.078125, ((1, 128),))
    up_weight = gaussian(arg_keys[8], (D, EXP_WIN * FFW), D ** -0.5, 0.078125, ((1, 128),))
    down_weight = gaussian(arg_keys[9], (EXP_WIN * FFW, D), FFW ** -0.5, 0.0625, ((0, 128),))
    return dict(queries=queries, key_rows=key_rows, value_rows=value_rows, segments=segments, swap_flags=swap_flags, expert_ids=expert_ids, norm_gain=norm_gain, gate_weight=gate_weight, up_weight=up_weight, down_weight=down_weight)


def attend(query_pack, key_pack, value_pack, segment_pack):
    length = query_pack.shape[0]
    group = HEADS // KVH
    query_f = query_pack.astype(jnp.float32).reshape(length, KVH, group, HD)
    key_f = key_pack.astype(jnp.float32).reshape(length, KVH, HD)
    value_f = value_pack.astype(jnp.float32).reshape(length, KVH, HD)
    scores = jnp.einsum('qhgd,khd->hgqk', query_f, key_f) * HD ** (-0.5)
    position = jnp.arange(length)
    allowed = (segment_pack[:, None] == segment_pack[None, :]) & (position[:, None] >= position[None, :])
    scores = jnp.where(allowed, scores, jnp.float32(-1e+30))
    top = lax.optimization_barrier(jnp.max(scores, -1, keepdims=True))
    expo = jnp.exp(scores - top)
    probs = (expo / lax.optimization_barrier(jnp.sum(expo, -1, keepdims=True))).astype(jnp.bfloat16)
    mixed = jnp.einsum('hgqk,khd->qhgd', probs.astype(jnp.float32), value_f)
    return mixed.reshape(length, HEADS * HD).astype(jnp.bfloat16)

def feed(rows, gate, upper, down):
    gate_out = jnp.dot(rows, gate, preferred_element_type=jnp.float32)
    up_out = jnp.dot(rows, upper, preferred_element_type=jnp.float32)
    hidden = (jax.nn.silu(gate_out) * up_out).astype(jnp.bfloat16)
    return jnp.dot(hidden, down, preferred_element_type=jnp.float32)

def reference(queries, key_rows, value_rows, segments, swap_flags, expert_ids, norm_gain, gate_weight, up_weight, down_weight):
    packs = N_DP * N_EXPERT
    flag = swap_flags > 0

    def place(array):
        shaped = array.reshape((N_DP, N_EXPERT, TOK_DEV, array.shape[-1]))
        return jnp.where(flag.reshape(1, N_EXPERT, 1, 1), shaped[::-1], shaped).reshape(packs, TOK_DEV, array.shape[-1])
    moved_q = place(queries)
    moved_k = place(key_rows)
    moved_v = place(value_rows)
    seg_shaped = segments.reshape(N_DP, N_EXPERT, TOK_DEV)
    moved_s = jnp.where(flag.reshape(1, N_EXPERT, 1), seg_shaped[::-1], seg_shaped).reshape(packs, TOK_DEV)
    attn = lax.map(lambda item: attend(item[0], item[1], item[2], item[3]), (moved_q, moved_k, moved_v, moved_s))
    attn_f = attn.astype(jnp.float32)
    scale = lax.rsqrt(lax.optimization_barrier(jnp.mean(attn_f * attn_f, -1, keepdims=True)) + 1e-05)
    normed = (attn_f * scale * norm_gain.astype(jnp.float32)).astype(jnp.bfloat16)
    route = expert_ids.reshape(packs, TOK_DEV)
    choose = (route[..., None] == jnp.arange(EXP_WIN, dtype=jnp.int32)).astype(jnp.int32)
    order = jnp.cumsum(choose, axis=1) - 1
    slot = lax.optimization_barrier(jnp.sum(choose * order, -1))
    disp = choose[..., None].astype(jnp.float32) * (slot[..., None, None] == jnp.arange(CAP, dtype=jnp.int32)).astype(jnp.float32)
    buffers = jnp.einsum('ntec,ntd->necd', disp, normed.astype(jnp.float32), precision=lax.Precision.HIGHEST).astype(jnp.bfloat16)

    def expert_block(index):
        rows = lax.dynamic_index_in_dim(buffers, index, 1, keepdims=False).reshape(packs * CAP, D)

        def add_shard(shard, total):
            shard = jnp.asarray(shard).astype(jnp.int32)
            start = ((index * SHARDS + shard) * FF_DEV).astype(jnp.int32)
            routed = feed(rows, lax.dynamic_slice_in_dim(gate_weight, start, FF_DEV, 1), lax.dynamic_slice_in_dim(up_weight, start, FF_DEV, 1), lax.dynamic_slice_in_dim(down_weight, start, FF_DEV, 0))
            rounded = lax.optimization_barrier(routed.astype(jnp.bfloat16))
            return total + rounded.astype(jnp.float32)
        total = lax.fori_loop(0, SHARDS, add_shard, jnp.zeros((packs * CAP, D), jnp.float32))
        return total.reshape(packs, CAP, D)
    results = lax.map(expert_block, jnp.arange(EXP_WIN, dtype=jnp.int32))
    experts_sum = jnp.einsum('ntec,encd->ntd', disp, results, precision=lax.Precision.HIGHEST)
    layer_out = (attn_f + experts_sum).astype(jnp.bfloat16)
    return layer_out.reshape(TOKENS, D)
```

```python
import functools
import itertools

import jax
import jax.numpy as jnp
from jax import lax
from jax.experimental import pallas as pl
from jax.experimental.pallas import tpu as pltpu
from jax.sharding import PartitionSpec as P

HEADS = 40
KVH = 8
GROUP = HEADS // KVH
HD = 128
D = 5120
FF = 256
EXP_WIN = 4
CAP = 10
TOK = 128
ROWS = EXP_WIN * CAP
LINE = 4 * ROWS
HALF = D // 2
ALL = ("dp", "expert")
MIB = 1 << 20
HINT = 6_000_000_000


def device_pairs(target):
    pairs = []
    for dp, z, y, x in itertools.product(range(2), range(8), range(4), range(4)):
        to = target(dp, z, y, x)
        pairs.append((((dp * 8 + z) * 4 + y) * 4 + x, ((to[0] * 8 + to[1]) * 4 + to[2]) * 4 + to[3]))
    return pairs


def plane_shift(phase, step):
    def target(dp, z, y, x):
        if (dp == 0) == (phase == 1):
            return dp, z, y, (x + step) % 4
        return dp, z, (y + step) % 4, x

    return device_pairs(target)


def to_expert(kind):
    offset = {1: (2, -2), 2: (-3, 3), 3: (-1, 1)}[kind]
    return device_pairs(lambda dp, z, y, x: (dp, (z + offset[z % 2]) % 8, y, x))


def reverse(pairs):
    return [(b, a) for a, b in pairs]


def send(value, pairs):
    return lax.ppermute(value, ALL, pairs)


def attention_kernel(info, q0, q1, k0, k1, v0, v1, bias_ref, route_ref, gain_ref, attn_ref, pick_ref, b0, b1, b2, b3, acc):
    moved = info[0] > 0
    bias = bias_ref[...]
    acc[...] = jnp.zeros_like(acc)
    for h in range(KVH):
        cols = slice(h * HD, (h + 1) * HD)
        key = jnp.where(moved, k1[:, cols], k0[:, cols])
        value = jnp.where(moved, v1[:, cols], v0[:, cols])
        heads = [slice((h * GROUP + g) * HD, (h * GROUP + g + 1) * HD) for g in range(GROUP)]
        query = jnp.concatenate([jnp.where(moved, q1[:, c], q0[:, c]) for c in heads], axis=0)
        scores = lax.dot_general(query, key, (((1,), (1,)), ((), ())), preferred_element_type=jnp.float32)
        scores = scores.reshape(GROUP, TOK, TOK) * HD ** (-0.5) + bias[None]
        top = jnp.max(scores, axis=-1, keepdims=True)
        expo = jnp.exp(scores - top)
        probs = (expo * (1.0 / jnp.sum(expo, axis=-1, keepdims=True))).astype(jnp.bfloat16)
        mixed = jnp.dot(probs.reshape(GROUP * TOK, TOK), value, preferred_element_type=jnp.float32)
        mixed = mixed.astype(jnp.bfloat16)
        for g, c in enumerate(heads):
            part = mixed[g * TOK:(g + 1) * TOK]
            attn_ref[:, c] = part
            part_f = part.astype(jnp.float32)
            acc[...] += part_f * part_f
    scale = lax.rsqrt(jnp.sum(acc[...], axis=-1, keepdims=True) * (1.0 / D) + 1e-05)
    route = route_ref[...]
    kind = jnp.where(route < EXP_WIN, ((route - info[1]) * info[2]) & 3, 64)
    lanes = lax.broadcasted_iota(jnp.int32, (TOK, TOK), 1)
    earlier = (lax.broadcasted_iota(jnp.int32, (TOK, TOK), 0) < lanes).astype(jnp.bfloat16)
    chosen = (lax.broadcasted_iota(jnp.int32, (16, TOK), 0) == kind).astype(jnp.bfloat16)
    order = jnp.dot(chosen, earlier, preferred_element_type=jnp.float32)
    slot = jnp.sum(chosen.astype(jnp.float32) * order, axis=0, keepdims=True).astype(jnp.int32)
    place = kind * 16 + slot
    pick = (lax.broadcasted_iota(jnp.int32, (64, TOK), 0) == place).astype(jnp.bfloat16)
    pick_ref[...] = pick
    for n in range(8):
        c = slice(n * 640, (n + 1) * 640)
        normed = (attn_ref[:, c].astype(jnp.float32) * scale * gain_ref[:, c].astype(jnp.float32)).astype(jnp.bfloat16)
        rows = jnp.dot(pick, normed, preferred_element_type=jnp.float32).astype(jnp.bfloat16)
        for i, b in enumerate((b0, b1, b2, b3)):
            b[:, c] = rows[i * 16:i * 16 + CAP]


def attention(info, q0, q1, k0, k1, v0, v1, bias, route, gain):
    vmem = pl.BlockSpec(memory_space=pltpu.VMEM)
    rows = jax.ShapeDtypeStruct((CAP, D), jnp.bfloat16)
    return pl.pallas_call(
        attention_kernel,
        out_shape=(
            jax.ShapeDtypeStruct((TOK, D), jnp.bfloat16),
            jax.ShapeDtypeStruct((64, TOK), jnp.bfloat16),
            rows, rows, rows, rows,
        ),
        in_specs=[pl.BlockSpec(memory_space=pltpu.SMEM)] + [vmem] * 9,
        out_specs=(vmem,) * 6,
        scratch_shapes=[pltpu.VMEM((TOK, TOK), jnp.float32)],
        compiler_params=pltpu.CompilerParams(vmem_limit_bytes=32 * MIB),
        cost_estimate=pl.CostEstimate(flops=400_000_000, bytes_accessed=6_000_000, transcendentals=660_000),
        name="attention",
    )(info, q0, q1, k0, k1, v0, v1, bias, route, gain)


def silu_mul(gate, up):
    return (gate / (1.0 + jnp.exp(-gate)) * up).astype(jnp.bfloat16)


def hidden_kernel(count, rows, parts, info, *refs):
    xs = refs[:count]
    n_w = len(refs) - count - 6
    srcs = list(refs[count:count + n_w])
    h_ref = refs[count + n_w]
    x_buf, g_buf, u_buf, x_sem, w_sem = refs[count + n_w + 1:]
    near = pl.multiple_of(info[3] * HALF, HALF)
    far = pl.multiple_of((1 - info[3]) * HALF, HALF)
    gate_loads, up_loads = [], []
    for i, part in enumerate(parts):
        for loads, buf in ((gate_loads, g_buf), (up_loads, u_buf)):
            if part == "own":
                loads.append([(srcs.pop(0), buf.at[i])])
            else:
                loads.append([(srcs.pop(0), buf.at[i, pl.ds(near, HALF)]), (srcs.pop(0), buf.at[i, pl.ds(far, HALF)])])
    x_copies = [pltpu.make_async_copy(x, x_buf.at[pl.ds(i * rows, rows)], x_sem.at[i]) for i, x in enumerate(xs)]
    for c in x_copies:
        c.start()
    sem = 0
    waits = []
    for pair in zip(gate_loads, up_loads):
        waits.append([])
        for loads in pair:
            copies = []
            for src, dst in loads:
                copies.append(pltpu.make_async_copy(src, dst, w_sem.at[sem]))
                copies[-1].start()
                sem += 1
            waits[-1].append(copies)
    for c in x_copies:
        c.wait()
    x = x_buf[...]
    for i in range(len(parts)):
        for c in waits[i][0]:
            c.wait()
        gate = jnp.dot(x, g_buf[i], preferred_element_type=jnp.float32)
        for c in waits[i][1]:
            c.wait()
        up = jnp.dot(x, u_buf[i], preferred_element_type=jnp.float32)
        h_ref[:, i * FF:(i + 1) * FF] = silu_mul(gate, up)


def hidden(info, xs, parts, weights, flops=0):
    count, rows, n = len(xs), xs[0].shape[0], len(parts)
    anyspec = pl.BlockSpec(memory_space=pl.ANY)
    total = count * rows
    return pl.pallas_call(
        functools.partial(hidden_kernel, count, rows, parts),
        out_shape=jax.ShapeDtypeStruct((total, n * FF), jnp.bfloat16),
        in_specs=[pl.BlockSpec(memory_space=pltpu.SMEM)] + [anyspec] * (count + len(weights)),
        out_specs=pl.BlockSpec(memory_space=pltpu.VMEM),
        scratch_shapes=[
            pltpu.VMEM((total, D), jnp.bfloat16),
            pltpu.VMEM((n, D, FF), jnp.bfloat16),
            pltpu.VMEM((n, D, FF), jnp.bfloat16),
            pltpu.SemaphoreType.DMA((count,)),
            pltpu.SemaphoreType.DMA((6,)),
        ],
        compiler_params=pltpu.CompilerParams(vmem_limit_bytes=28 * MIB),
        cost_estimate=pl.CostEstimate(flops=max(flops, 4 * total * D * n * FF), bytes_accessed=4 * D * n * FF + 2 * total * D, transcendentals=total * n * FF),
        name="hidden",
    )(info, *xs, *weights)


def down_kernel(layout, info, *refs):
    hs = refs[:len(layout)]
    own_w, wa, wb = refs[len(layout):len(layout) + 3]
    o0, o1, o2, o3, h_buf, w_buf, y_buf, h_sem, w_sem, y_sem = refs[len(layout) + 3:]
    wn = pl.multiple_of(info[3] * (FF // 2) + FF, FF // 2)
    wf = pl.multiple_of((1 - info[3]) * (FF // 2) + FF, FF // 2)
    copies = [
        pltpu.make_async_copy(own_w, w_buf.at[pl.ds(0, FF)], w_sem.at[0]),
        pltpu.make_async_copy(wa, w_buf.at[pl.ds(wn, FF // 2)], w_sem.at[1]),
        pltpu.make_async_copy(wb, w_buf.at[pl.ds(wf, FF // 2)], w_sem.at[2]),
    ]
    for i, (h, (row, col)) in enumerate(zip(hs, layout)):
        to = h_buf.at[pl.ds(row, h.shape[0]), pl.ds(col, h.shape[1])]
        copies.append(pltpu.make_async_copy(h, to, h_sem.at[i]))
    for c in copies:
        c.start()
    for c in copies:
        c.wait()
    tile = 512
    outs = []
    for i, o in ((3, o3), (1, o1), (2, o2), (0, o0)):
        rows = pl.ds(i * LINE, LINE)

        @pl.loop(0, y_buf.shape[1] // tile)
        def _(n):
            cols = pl.ds(pl.multiple_of(n * tile, tile), tile)
            y_buf[rows, cols] = jnp.dot(h_buf[rows, :], w_buf[:, cols], preferred_element_type=jnp.float32).astype(jnp.bfloat16)

        c = pltpu.make_async_copy(y_buf.at[rows], o, y_sem.at[i])
        c.start()
        outs.append(c)
    for c in outs:
        c.wait()


def down(info, hs, layout, own_w, wa, wb):
    anyspec = pl.BlockSpec(memory_space=pl.ANY)
    width = own_w.shape[1]
    total = 4 * LINE
    return pl.pallas_call(
        functools.partial(down_kernel, layout),
        out_shape=tuple(jax.ShapeDtypeStruct((LINE, width), jnp.bfloat16) for _ in range(4)),
        in_specs=[pl.BlockSpec(memory_space=pltpu.SMEM)] + [anyspec] * (len(hs) + 3),
        out_specs=(anyspec,) * 4,
        scratch_shapes=[
            pltpu.VMEM((total, 2 * FF), jnp.bfloat16),
            pltpu.VMEM((2 * FF, width), jnp.bfloat16),
            pltpu.VMEM((total, width), jnp.bfloat16),
            pltpu.SemaphoreType.DMA((len(hs),)),
            pltpu.SemaphoreType.DMA((3,)),
            pltpu.SemaphoreType.DMA((4,)),
        ],
        compiler_params=pltpu.CompilerParams(vmem_limit_bytes=24 * MIB),
        cost_estimate=pl.CostEstimate(flops=2 * total * 2 * FF * width, bytes_accessed=4 * FF * width + 2 * total * width, transcendentals=0),
        name="down",
    )(info, *hs, own_w, wa, wb)


def combine_kernel(pick_ref, attn_ref, r0, r1, r2, r3, out_ref):
    for n in range(8):
        c = slice(n * 640, (n + 1) * 640)
        total = attn_ref[:, c].astype(jnp.float32)
        for i, r in enumerate((r0, r1, r2, r3)):
            total += lax.dot_general(
                pick_ref[i * 16:i * 16 + CAP], r[:, c], (((0,), (0,)), ((), ())), preferred_element_type=jnp.float32
            )
        out_ref[:, c] = total.astype(jnp.bfloat16)


def combine(pick, attn, rows):
    vmem = pl.BlockSpec(memory_space=pltpu.VMEM)
    return pl.pallas_call(
        combine_kernel,
        out_shape=jax.ShapeDtypeStruct((TOK, D), jnp.bfloat16),
        in_specs=[vmem] * 6,
        out_specs=vmem,
        compiler_params=pltpu.CompilerParams(vmem_limit_bytes=32 * MIB),
        cost_estimate=pl.CostEstimate(flops=60_000_000, bytes_accessed=3_000_000, transcendentals=0),
        name="combine",
    )(pick, attn, *rows)


def add_up(parts):
    total = parts[0].astype(jnp.float32)
    for p in parts[1:]:
        total = total + p.astype(jnp.float32)
    return total.astype(jnp.bfloat16)


def after(value, *others):
    return lax.optimization_barrier((value, others))[0]


def per_device(queries, key_rows, value_rows, segments, swap_flags, expert_ids, norm_gain, gate_weight, up_weight, down_weight):
    dp = lax.axis_index("dp")
    z = lax.axis_index("expert") // 16
    info = jnp.stack([swap_flags[0], z // 2, 1 - 2 * (z % 2), dp]).astype(jnp.int32)

    across = device_pairs(lambda d, zz, y, x: (d, zz ^ 1, y, x))
    beside = device_pairs(lambda d, zz, y, x: (1 - d, zz, y, x))
    gu_a = send(
        jnp.concatenate([lax.dynamic_slice_in_dim(w, dp * HALF, HALF, 0) for w in (gate_weight, up_weight)], axis=0),
        across,
    )

    seg_local = segments.astype(jnp.bfloat16)
    q1, k1, v1, s1 = (send(a, beside) for a in (queries, key_rows, value_rows, seg_local))
    seg = jnp.where(swap_flags[0] > 0, s1, seg_local)[0].astype(jnp.float32)
    position = jnp.arange(TOK)
    allowed = (seg[:, None] == seg[None, :]) & (position[:, None] >= position[None, :])
    bias = jnp.where(allowed, jnp.float32(0), jnp.float32(-1e30))
    attn, pick, *rows = attention(
        info, queries, q1, key_rows, k1, value_rows, v1, bias, expert_ids.reshape(1, TOK), norm_gain.reshape(1, D)
    )

    mine = jnp.concatenate([rows[0]] + [send(rows[k], to_expert(k)) for k in (1, 2, 3)], axis=0)
    w_cols = [down_weight[:, :HALF], down_weight[:, HALF:]]
    line = jnp.concatenate([mine] + [send(mine, plane_shift(1, s)) for s in (1, 3, 2)], axis=0)
    c1, c3, c2 = (send(line, plane_shift(2, s)) for s in (1, 3, 2))

    own_gu = (gate_weight, up_weight)
    h_line = hidden(info, [line], ("own",), own_gu)
    gu_a = after(gu_a, h_line)
    ga, ua = gu_a[:HALF], gu_a[HALF:]
    other_gu = (ga, send(ga, beside), ua, send(ua, beside))
    h_near = hidden(info, [c1, c3], ("own",), own_gu, HINT)
    wa = []
    for w, first in zip(w_cols, (line, h_near)):
        start = after(dp, first) * (FF // 2)
        wa.append(send(lax.dynamic_slice_in_dim(w, start, FF // 2, 0), across))
    h_other = hidden(info, [after(line, h_near), c1, c3], ("other",), other_gu)
    wa[0] = after(wa[0], h_other)
    wb0 = send(wa[0], beside)
    h_last = hidden(info, [after(c2, h_other)], ("own", "other"), own_gu + other_gu, 2 * HINT)
    hs = (h_line, h_near, h_other, h_last)
    layout = ((0, 0), (LINE, 0), (0, FF), (3 * LINE, 0))

    def spread(outs):
        return [outs[0]] + [send(o, plane_shift(2, s)) for o, s in zip(outs[1:], (3, 1, 2))]

    def line_sums(parts):
        back = [add_up([p[i * ROWS:(i + 1) * ROWS] for p in parts]) for i in range(4)]
        return [back[0]] + [send(b, plane_shift(1, s)) for b, s in zip(back[1:], (3, 1, 2))]

    outs0 = down(info, hs, layout, w_cols[0], wa[0], wb0)
    parts0 = spread(outs0)
    wa[1] = after(wa[1], outs0[0])
    outs1 = down(info, hs, layout, w_cols[1], wa[1], send(wa[1], beside))
    parts1 = spread(outs1)
    sums0 = line_sums(after(parts0, outs1[0]))
    sums1 = line_sums(parts1)
    mine_sum = jnp.concatenate([add_up(sums0), add_up(sums1)], axis=1)
    pieces = [mine_sum[k * CAP:(k + 1) * CAP] for k in range(4)]
    returned = [pieces[0]] + [send(pieces[k], reverse(to_expert(k))) for k in (1, 2, 3)]
    return combine(pick, attn, returned)


def solution(mesh):
    in_specs = (
        P(("dp", "expert"), None),
        P(("dp", "expert"), None),
        P(("dp", "expert"), None),
        P(("dp", "expert"), None),
        P("expert"),
        P(("dp", "expert"), None),
        P(),
        P(None, "expert"),
        P(None, "expert"),
        P("expert", None),
    )
    out_specs = P(("dp", "expert"), None)
    return jax.shard_map(
        per_device, mesh=mesh, in_specs=in_specs, out_specs=out_specs, check_vma=False
    )
```

```python
import functools
import itertools

import jax
import jax.numpy as jnp
from jax import lax
from jax.experimental import pallas as pl
from jax.experimental.pallas import tpu as pltpu
from jax.sharding import PartitionSpec as P

HEADS = 40
KVH = 8
GROUP = HEADS // KVH
HD = 128
D = 5120
FF = 256
EXP_WIN = 4
CAP = 10
TOK = 128
ROWS = EXP_WIN * CAP
LINE = 4 * ROWS
HALF = D // 2
CUT = 1536
ALL = ("dp", "expert")
MIB = 1 << 20
HINT = 6_000_000_000


def device_pairs(target):
    pairs = []
    for dp, z, y, x in itertools.product(range(2), range(8), range(4), range(4)):
        to = target(dp, z, y, x)
        pairs.append((((dp * 8 + z) * 4 + y) * 4 + x, ((to[0] * 8 + to[1]) * 4 + to[2]) * 4 + to[3]))
    return pairs


def plane_shift(phase, step):
    def target(dp, z, y, x):
        if (dp == 0) == (phase == 1):
            return dp, z, y, (x + step) % 4
        return dp, z, (y + step) % 4, x

    return device_pairs(target)


def to_expert(kind):
    offset = {1: (2, -2), 2: (-3, 3), 3: (-1, 1)}[kind]
    return device_pairs(lambda dp, z, y, x: (dp, (z + offset[z % 2]) % 8, y, x))


def reverse(pairs):
    return [(b, a) for a, b in pairs]


def send(value, pairs):
    return lax.ppermute(value, ALL, pairs)


def attention_kernel(info, q0, q1, k0, k1, v0, v1, bias_ref, route_ref, gain_ref, attn_ref, pick_ref, b0, b1, b2, b3, acc):
    moved = info[0] > 0
    bias = bias_ref[...]
    acc[...] = jnp.zeros_like(acc)
    for h in range(KVH):
        cols = slice(h * HD, (h + 1) * HD)
        key = jnp.where(moved, k1[:, cols], k0[:, cols])
        value = jnp.where(moved, v1[:, cols], v0[:, cols])
        heads = [slice((h * GROUP + g) * HD, (h * GROUP + g + 1) * HD) for g in range(GROUP)]
        query = jnp.concatenate([jnp.where(moved, q1[:, c], q0[:, c]) for c in heads], axis=0)
        scores = lax.dot_general(query, key, (((1,), (1,)), ((), ())), preferred_element_type=jnp.float32)
        scores = scores.reshape(GROUP, TOK, TOK) * HD ** (-0.5) + bias[None]
        top = jnp.max(scores, axis=-1, keepdims=True)
        expo = jnp.exp(scores - top)
        probs = (expo * (1.0 / jnp.sum(expo, axis=-1, keepdims=True))).astype(jnp.bfloat16)
        mixed = jnp.dot(probs.reshape(GROUP * TOK, TOK), value, preferred_element_type=jnp.float32)
        mixed = mixed.astype(jnp.bfloat16)
        for g, c in enumerate(heads):
            part = mixed[g * TOK:(g + 1) * TOK]
            attn_ref[:, c] = part
            part_f = part.astype(jnp.float32)
            acc[...] += part_f * part_f
    scale = lax.rsqrt(jnp.sum(acc[...], axis=-1, keepdims=True) * (1.0 / D) + 1e-05)
    route = route_ref[...]
    kind = jnp.where(route < EXP_WIN, ((route - info[1]) * info[2]) & 3, 64)
    lanes = lax.broadcasted_iota(jnp.int32, (TOK, TOK), 1)
    earlier = (lax.broadcasted_iota(jnp.int32, (TOK, TOK), 0) < lanes).astype(jnp.bfloat16)
    chosen = (lax.broadcasted_iota(jnp.int32, (16, TOK), 0) == kind).astype(jnp.bfloat16)
    order = jnp.dot(chosen, earlier, preferred_element_type=jnp.float32)
    slot = jnp.sum(chosen.astype(jnp.float32) * order, axis=0, keepdims=True).astype(jnp.int32)
    place = kind * 16 + slot
    pick = (lax.broadcasted_iota(jnp.int32, (64, TOK), 0) == place).astype(jnp.bfloat16)
    pick_ref[...] = pick
    for n in range(8):
        c = slice(n * 640, (n + 1) * 640)
        normed = (attn_ref[:, c].astype(jnp.float32) * scale * gain_ref[:, c].astype(jnp.float32)).astype(jnp.bfloat16)
        rows = jnp.dot(pick, normed, preferred_element_type=jnp.float32).astype(jnp.bfloat16)
        for i, b in enumerate((b0, b1, b2, b3)):
            b[:, c] = rows[i * 16:i * 16 + CAP]


def attention(info, q0, q1, k0, k1, v0, v1, bias, route, gain):
    vmem = pl.BlockSpec(memory_space=pltpu.VMEM)
    rows = jax.ShapeDtypeStruct((CAP, D), jnp.bfloat16)
    return pl.pallas_call(
        attention_kernel,
        out_shape=(
            jax.ShapeDtypeStruct((TOK, D), jnp.bfloat16),
            jax.ShapeDtypeStruct((64, TOK), jnp.bfloat16),
            rows, rows, rows, rows,
        ),
        in_specs=[pl.BlockSpec(memory_space=pltpu.SMEM)] + [vmem] * 9,
        out_specs=(vmem,) * 6,
        scratch_shapes=[pltpu.VMEM((TOK, TOK), jnp.float32)],
        compiler_params=pltpu.CompilerParams(vmem_limit_bytes=32 * MIB),
        cost_estimate=pl.CostEstimate(flops=400_000_000, bytes_accessed=6_000_000, transcendentals=660_000),
        name="attention",
    )(info, q0, q1, k0, k1, v0, v1, bias, route, gain)


def silu_mul(gate, up):
    return (gate / (1.0 + jnp.exp(-gate)) * up).astype(jnp.bfloat16)


def hidden_kernel(count, parts, info, *refs):
    xs = refs[:count]
    n_w = len(refs) - count - 4
    srcs = list(refs[count:count + n_w])
    h_ref, g_buf, u_buf, sem = refs[count + n_w:]
    near = info[3] * HALF
    far = HALF - near
    plans = []
    for i, part in enumerate(parts):
        for which, buf in enumerate((g_buf, u_buf)):
            if part == "own":
                src = srcs.pop(0)
                loads = [(src.at[pl.ds(k, n)], k, n) for k, n in ((0, CUT), (CUT, HALF - CUT), (HALF, CUT), (HALF + CUT, HALF - CUT))]
            elif which == 0:
                a1, a2, b1, b2 = (srcs.pop(0) for _ in range(4))
                loads = [(a1, near, CUT), (b1, far, CUT), (a2, near + CUT, HALF - CUT), (b2, far + CUT, HALF - CUT)]
            else:
                loads = [(srcs.pop(0), near, HALF), (srcs.pop(0), far, HALF)]
            plan = []
            for j, (src, k, n) in enumerate(loads):
                at = pl.ds(k if isinstance(k, int) else pl.multiple_of(k, HD), n)
                copy = pltpu.make_async_copy(src, buf.at[i, at], sem.at[i, which, j])
                copy.start()
                plan.append((copy, at))
            plans.append(plan)
    for i in range(len(parts)):
        sums = []
        for which, buf in enumerate((g_buf, u_buf)):
            total = None
            for copy, at in plans[2 * i + which]:
                copy.wait()
                x = jnp.concatenate([r[:, at] for r in xs], axis=0)
                term = jnp.dot(x, buf[i, at, :], preferred_element_type=jnp.float32)
                total = term if total is None else total + term
            sums.append(total)
        h_ref[:, i * FF:(i + 1) * FF] = silu_mul(*sums)


def hidden(info, xs, parts, weights, flops=0):
    count, rows, n = len(xs), xs[0].shape[0], len(parts)
    hbm, vmem = pl.BlockSpec(memory_space=pltpu.HBM), pl.BlockSpec(memory_space=pltpu.VMEM)
    total = count * rows
    return pl.pallas_call(
        functools.partial(hidden_kernel, count, parts),
        out_shape=jax.ShapeDtypeStruct((total, n * FF), jnp.bfloat16),
        in_specs=[pl.BlockSpec(memory_space=pltpu.SMEM)] + [vmem] * count + [hbm] * len(weights),
        out_specs=vmem,
        scratch_shapes=[
            pltpu.VMEM((n, D, FF), jnp.bfloat16),
            pltpu.VMEM((n, D, FF), jnp.bfloat16),
            pltpu.SemaphoreType.DMA((n, 2, 4)),
        ],
        compiler_params=pltpu.CompilerParams(vmem_limit_bytes=28 * MIB),
        cost_estimate=pl.CostEstimate(flops=max(flops, 4 * total * D * n * FF), bytes_accessed=4 * D * n * FF + 2 * total * D, transcendentals=total * n * FF),
        name="hidden",
    )(info, *xs, *weights)


def down_kernel(first, tile, info, h_line, h_near, h_other, h_last, own_w, wa, wb, o0, o1, o2, o3, w_buf, sem):
    width = w_buf.shape[1]
    wn = pl.multiple_of(info[3] * (FF // 2) + FF, FF // 2)
    wf = pl.multiple_of((1 - info[3]) * (FF // 2) + FF, FF // 2)
    copies = []
    for n in range(width // tile):
        cols = pl.ds(n * tile, tile)
        copies.append([
            pltpu.make_async_copy(own_w.at[:, pl.ds(first + n * tile, tile)], w_buf.at[pl.ds(0, FF), cols], sem.at[n, 0]),
            pltpu.make_async_copy(wa.at[:, cols], w_buf.at[pl.ds(wn, FF // 2), cols], sem.at[n, 1]),
            pltpu.make_async_copy(wb.at[:, cols], w_buf.at[pl.ds(wf, FF // 2), cols], sem.at[n, 2]),
        ])
        for c in copies[-1]:
            c.start()
    own = jnp.concatenate([h_line[...], h_near[...], h_last[:, :FF]], axis=0)
    other = jnp.concatenate([h_other[...], h_last[:, FF:]], axis=0)
    h = jnp.concatenate([own, other], axis=1)
    for n in range(width // tile):
        cols = pl.ds(n * tile, tile)
        for c in copies[n]:
            c.wait()
        y = jnp.dot(h, w_buf[:, cols], preferred_element_type=jnp.float32).astype(jnp.bfloat16)
        for i, o in enumerate((o0, o1, o2, o3)):
            o[:, cols] = y[i * LINE:(i + 1) * LINE]


def down(info, hs, first, own_w, wa, wb):
    hbm, vmem = pl.BlockSpec(memory_space=pltpu.HBM), pl.BlockSpec(memory_space=pltpu.VMEM)
    width = wa.shape[1]
    tile = 512
    total = 4 * LINE
    return pl.pallas_call(
        functools.partial(down_kernel, first, tile),
        out_shape=tuple(jax.ShapeDtypeStruct((LINE, width), jnp.bfloat16) for _ in range(4)),
        in_specs=[pl.BlockSpec(memory_space=pltpu.SMEM)] + [vmem] * len(hs) + [hbm] * 3,
        out_specs=(vmem,) * 4,
        scratch_shapes=[
            pltpu.VMEM((2 * FF, width), jnp.bfloat16),
            pltpu.SemaphoreType.DMA((width // tile, 3)),
        ],
        compiler_params=pltpu.CompilerParams(vmem_limit_bytes=24 * MIB),
        cost_estimate=pl.CostEstimate(flops=2 * total * 2 * FF * width, bytes_accessed=4 * FF * width + 2 * total * width, transcendentals=0),
        name="down",
    )(info, *hs, own_w, wa, wb)


def stack_kernel(*refs):
    at = 0
    for r in refs[:-1]:
        refs[-1][at:at + r.shape[0], :] = r[...]
        at += r.shape[0]


def stack(parts):
    vmem = pl.BlockSpec(memory_space=pltpu.VMEM)
    rows = sum(p.shape[0] for p in parts)
    return pl.pallas_call(
        stack_kernel,
        out_shape=jax.ShapeDtypeStruct((rows, D), jnp.bfloat16),
        in_specs=[vmem] * len(parts),
        out_specs=vmem,
        compiler_params=pltpu.CompilerParams(vmem_limit_bytes=16 * MIB),
        cost_estimate=pl.CostEstimate(flops=0, bytes_accessed=4 * rows * D, transcendentals=0),
        name="stack",
    )(*parts)


def combine_kernel(pick_ref, attn_ref, r0, r1, r2, r3, out_ref):
    for n in range(8):
        c = slice(n * 640, (n + 1) * 640)
        total = attn_ref[:, c].astype(jnp.float32)
        for i, r in enumerate((r0, r1, r2, r3)):
            total += lax.dot_general(
                pick_ref[i * 16:i * 16 + CAP], r[:, c], (((0,), (0,)), ((), ())), preferred_element_type=jnp.float32
            )
        out_ref[:, c] = total.astype(jnp.bfloat16)


def combine(pick, attn, rows):
    vmem = pl.BlockSpec(memory_space=pltpu.VMEM)
    return pl.pallas_call(
        combine_kernel,
        out_shape=jax.ShapeDtypeStruct((TOK, D), jnp.bfloat16),
        in_specs=[vmem] * 6,
        out_specs=vmem,
        compiler_params=pltpu.CompilerParams(vmem_limit_bytes=32 * MIB),
        cost_estimate=pl.CostEstimate(flops=60_000_000, bytes_accessed=3_000_000, transcendentals=0),
        name="combine",
    )(pick, attn, *rows)


def add_up(parts):
    total = parts[0].astype(jnp.float32)
    for p in parts[1:]:
        total = total + p.astype(jnp.float32)
    return total.astype(jnp.bfloat16)


def after(value, *others):
    return lax.optimization_barrier((value, others))[0]


def per_device(queries, key_rows, value_rows, segments, swap_flags, expert_ids, norm_gain, gate_weight, up_weight, down_weight):
    dp = lax.axis_index("dp")
    z = lax.axis_index("expert") // 16
    info = jnp.stack([swap_flags[0], z // 2, 1 - 2 * (z % 2), dp]).astype(jnp.int32)

    across = device_pairs(lambda d, zz, y, x: (d, zz ^ 1, y, x))
    beside = device_pairs(lambda d, zz, y, x: (1 - d, zz, y, x))
    g_first = send(lax.dynamic_slice_in_dim(gate_weight, dp * HALF, CUT, 0), across)

    seg_local = segments.astype(jnp.bfloat16)
    q1, k1, v1, s1 = (send(a, beside) for a in (queries, key_rows, value_rows, seg_local))
    seg = jnp.where(swap_flags[0] > 0, s1, seg_local)[0].astype(jnp.float32)
    position = jnp.arange(TOK)
    allowed = (seg[:, None] == seg[None, :]) & (position[:, None] >= position[None, :])
    bias = jnp.where(allowed, jnp.float32(0), jnp.float32(-1e30))
    attn, pick, *rows = attention(
        info, queries, q1, key_rows, k1, value_rows, v1, bias, expert_ids.reshape(1, TOK), norm_gain.reshape(1, D)
    )

    moved = [send(rows[k], to_expert(k)) for k in (1, 2, 3)]
    mine = jnp.concatenate([rows[0]] + after(moved, g_first), axis=0)
    g_rest = lax.dynamic_slice_in_dim(gate_weight, dp * HALF + CUT, HALF - CUT, 0)
    g_rest = send(after(g_rest, moved), across)
    line = stack([mine] + [send(mine, plane_shift(1, s)) for s in (1, 3, 2)])
    line_out = after(line, g_rest)
    c1, c3, c2 = (send(line_out, plane_shift(2, s)) for s in (1, 3, 2))
    u_half = lax.dynamic_slice_in_dim(up_weight, dp * HALF, HALF, 0)
    u_half = send(after(u_half, line_out), across)

    own_gu = (gate_weight, up_weight)
    h_line = hidden(info, [line], ("own",), own_gu)
    g_first, g_rest, u_half = after((g_first, g_rest, u_half), h_line)
    other_gu = (g_first, g_rest, send(g_first, beside), send(g_rest, beside), u_half, send(u_half, beside))
    h_near = hidden(info, [c1, c3], ("own",), own_gu, HINT)
    wa = []
    for col in (0, HALF):
        w = lax.dynamic_slice(down_weight, (dp * (FF // 2), col), (FF // 2, HALF))
        wa.append(send(after(w, line_out), across))
    h_other = hidden(info, [after(line, (h_near, wa[0])), c1, c3], ("other",), other_gu)
    wb0 = send(after(wa[0], h_near), beside)
    h_last = hidden(info, [after(c2, h_other)], ("own", "other"), own_gu + other_gu, 2 * HINT)
    hs = (h_line, h_near, h_other, h_last)

    def spread(outs):
        return [outs[0]] + [send(o, plane_shift(2, s)) for o, s in zip(outs[1:], (3, 1, 2))]

    def line_sums(parts):
        back = [add_up([p[i * ROWS:(i + 1) * ROWS] for p in parts]) for i in range(4)]
        return [back[0]] + [send(b, plane_shift(1, s)) for b, s in zip(back[1:], (3, 1, 2))]

    outs0 = down(info, hs, 0, down_weight, wa[0], wb0)
    parts0 = spread(outs0)
    wa[1] = after(wa[1], outs0[0])
    outs1 = down(info, hs, HALF, down_weight, wa[1], send(wa[1], beside))
    parts1 = spread(outs1)
    sums0 = line_sums(after(parts0, outs1[0]))
    sums1 = line_sums(parts1)
    mine_sum = jnp.concatenate([add_up(sums0), add_up(sums1)], axis=1)
    pieces = [mine_sum[k * CAP:(k + 1) * CAP] for k in range(4)]
    returned = [pieces[0]] + [send(pieces[k], reverse(to_expert(k))) for k in (1, 2, 3)]
    return combine(pick, attn, returned)


def solution(mesh):
    in_specs = (
        P(("dp", "expert"), None),
        P(("dp", "expert"), None),
        P(("dp", "expert"), None),
        P(("dp", "expert"), None),
        P("expert"),
        P(("dp", "expert"), None),
        P(),
        P(None, "expert"),
        P(None, "expert"),
        P("expert", None),
    )
    out_specs = P(("dp", "expert"), None)
    return jax.shard_map(
        per_device, mesh=mesh, in_specs=in_specs, out_specs=out_specs, check_vma=False
    )
```

```python
import functools
import itertools

import jax
import jax.numpy as jnp
from jax import lax
from jax.experimental import pallas as pl
from jax.experimental.pallas import tpu as pltpu
from jax.sharding import PartitionSpec as P

HEADS = 40
KVH = 8
GROUP = HEADS // KVH
HD = 128
D = 5120
FF = 256
EXP_WIN = 4
CAP = 10
TOK = 128
ROWS = EXP_WIN * CAP
LINE = 4 * ROWS
HALF = D // 2
CUT = 1280
ALL = ("dp", "expert")
MIB = 1 << 20
HINT = 6_000_000_000


def device_pairs(target):
    pairs = []
    for dp, z, y, x in itertools.product(range(2), range(8), range(4), range(4)):
        to = target(dp, z, y, x)
        pairs.append((((dp * 8 + z) * 4 + y) * 4 + x, ((to[0] * 8 + to[1]) * 4 + to[2]) * 4 + to[3]))
    return pairs


def plane_shift(phase, step):
    def target(dp, z, y, x):
        if (dp == 0) == (phase == 1):
            return dp, z, y, (x + step) % 4
        return dp, z, (y + step) % 4, x

    return device_pairs(target)


def to_expert(kind):
    offset = {1: (2, -2), 2: (-3, 3), 3: (-1, 1)}[kind]
    return device_pairs(lambda dp, z, y, x: (dp, (z + offset[z % 2]) % 8, y, x))


def reverse(pairs):
    return [(b, a) for a, b in pairs]


def send(value, pairs):
    return lax.ppermute(value, ALL, pairs)


def attention_kernel(info, q0, q1, k0, k1, v0, v1, bias_ref, route_ref, gain_ref, attn_ref, pick_ref, b0, b1, b2, b3, acc):
    moved = info[0] > 0
    bias = bias_ref[...]
    acc[...] = jnp.zeros_like(acc)
    for h in range(KVH):
        cols = slice(h * HD, (h + 1) * HD)
        key = jnp.where(moved, k1[:, cols], k0[:, cols])
        value = jnp.where(moved, v1[:, cols], v0[:, cols])
        heads = [slice((h * GROUP + g) * HD, (h * GROUP + g + 1) * HD) for g in range(GROUP)]
        query = jnp.concatenate([jnp.where(moved, q1[:, c], q0[:, c]) for c in heads], axis=0)
        scores = lax.dot_general(query, key, (((1,), (1,)), ((), ())), preferred_element_type=jnp.float32)
        scores = scores.reshape(GROUP, TOK, TOK) * HD ** (-0.5) + bias[None]
        top = jnp.max(scores, axis=-1, keepdims=True)
        expo = jnp.exp(scores - top)
        probs = (expo * (1.0 / jnp.sum(expo, axis=-1, keepdims=True))).astype(jnp.bfloat16)
        mixed = jnp.dot(probs.reshape(GROUP * TOK, TOK), value, preferred_element_type=jnp.float32)
        mixed = mixed.astype(jnp.bfloat16)
        for g, c in enumerate(heads):
            part = mixed[g * TOK:(g + 1) * TOK]
            attn_ref[:, c] = part
            part_f = part.astype(jnp.float32)
            acc[...] += part_f * part_f
    scale = lax.rsqrt(jnp.sum(acc[...], axis=-1, keepdims=True) * (1.0 / D) + 1e-05)
    route = route_ref[...]
    kind = jnp.where(route < EXP_WIN, ((route - info[1]) * info[2]) & 3, 64)
    lanes = lax.broadcasted_iota(jnp.int32, (TOK, TOK), 1)
    earlier = (lax.broadcasted_iota(jnp.int32, (TOK, TOK), 0) < lanes).astype(jnp.bfloat16)
    chosen = (lax.broadcasted_iota(jnp.int32, (16, TOK), 0) == kind).astype(jnp.bfloat16)
    order = jnp.dot(chosen, earlier, preferred_element_type=jnp.float32)
    slot = jnp.sum(chosen.astype(jnp.float32) * order, axis=0, keepdims=True).astype(jnp.int32)
    place = kind * 16 + slot
    pick = (lax.broadcasted_iota(jnp.int32, (64, TOK), 0) == place).astype(jnp.bfloat16)
    pick_ref[...] = pick
    for n in range(8):
        c = slice(n * 640, (n + 1) * 640)
        normed = (attn_ref[:, c].astype(jnp.float32) * scale * gain_ref[:, c].astype(jnp.float32)).astype(jnp.bfloat16)
        rows = jnp.dot(pick, normed, preferred_element_type=jnp.float32).astype(jnp.bfloat16)
        for i, b in enumerate((b0, b1, b2, b3)):
            b[:, c] = rows[i * 16:i * 16 + CAP]


def attention(info, q0, q1, k0, k1, v0, v1, bias, route, gain):
    vmem = pl.BlockSpec(memory_space=pltpu.VMEM)
    rows = jax.ShapeDtypeStruct((CAP, D), jnp.bfloat16)
    return pl.pallas_call(
        attention_kernel,
        out_shape=(
            jax.ShapeDtypeStruct((TOK, D), jnp.bfloat16),
            jax.ShapeDtypeStruct((64, TOK), jnp.bfloat16),
            rows, rows, rows, rows,
        ),
        in_specs=[pl.BlockSpec(memory_space=pltpu.SMEM)] + [vmem] * 9,
        out_specs=(vmem,) * 6,
        scratch_shapes=[pltpu.VMEM((TOK, TOK), jnp.float32)],
        compiler_params=pltpu.CompilerParams(vmem_limit_bytes=32 * MIB),
        cost_estimate=pl.CostEstimate(flops=400_000_000, bytes_accessed=6_000_000, transcendentals=660_000),
        name="attention",
    )(info, q0, q1, k0, k1, v0, v1, bias, route, gain)


def silu_mul(gate, up):
    return (gate / (1.0 + jnp.exp(-gate)) * up).astype(jnp.bfloat16)


def hidden_kernel(count, parts, info, *refs):
    xs = refs[:count]
    n_w = len(refs) - count - 3
    srcs = list(refs[count:count + n_w])
    h_ref, w_buf, sem = refs[count + n_w:]
    near = info[3] * HALF
    far = HALF - near
    plans = []
    for i, part in enumerate(parts):
        if part == "own":
            g, u = (srcs.pop(0) for _ in range(2))
            loads = [(g.at[pl.ds(k, CUT)], u.at[pl.ds(k, CUT)], k) for k in range(0, D, CUT)]
        else:
            ga1, ga2, gb1, gb2, ua, ub = (srcs.pop(0) for _ in range(6))
            head, tail = pl.ds(0, CUT), pl.ds(CUT, CUT)
            loads = [
                (ga1, ua.at[head], near),
                (gb1, ub.at[head], far),
                (ga2, ua.at[tail], near + CUT),
                (gb2, ub.at[tail], far + CUT),
            ]
        plan = []
        for j, (g, u, k) in enumerate(loads):
            at = pl.ds(k if isinstance(k, int) else pl.multiple_of(k, HD), CUT)
            copies = [
                pltpu.make_async_copy(g, w_buf.at[i, at, pl.ds(0, FF)], sem.at[i, 0, j]),
                pltpu.make_async_copy(u, w_buf.at[i, at, pl.ds(FF, FF)], sem.at[i, 1, j]),
            ]
            for c in copies:
                c.start()
            plan.append((copies, at))
        plans.append(plan)
    for i, plan in enumerate(plans):
        total = None
        for copies, at in plan:
            for c in copies:
                c.wait()
            x = jnp.concatenate([r[:, at] for r in xs], axis=0)
            term = jnp.dot(x, w_buf[i, at, :], preferred_element_type=jnp.float32)
            total = term if total is None else total + term
        h_ref[:, i * FF:(i + 1) * FF] = silu_mul(total[:, :FF], total[:, FF:])


def hidden(info, xs, parts, weights, flops=0):
    count, rows, n = len(xs), xs[0].shape[0], len(parts)
    hbm, vmem = pl.BlockSpec(memory_space=pltpu.HBM), pl.BlockSpec(memory_space=pltpu.VMEM)
    total = count * rows
    return pl.pallas_call(
        functools.partial(hidden_kernel, count, parts),
        out_shape=jax.ShapeDtypeStruct((total, n * FF), jnp.bfloat16),
        in_specs=[pl.BlockSpec(memory_space=pltpu.SMEM)] + [vmem] * count + [hbm] * len(weights),
        out_specs=vmem,
        scratch_shapes=[
            pltpu.VMEM((n, D, 2 * FF), jnp.bfloat16),
            pltpu.SemaphoreType.DMA((n, 2, 4)),
        ],
        compiler_params=pltpu.CompilerParams(vmem_limit_bytes=28 * MIB),
        cost_estimate=pl.CostEstimate(flops=max(flops, 4 * total * D * n * FF), bytes_accessed=4 * D * n * FF + 2 * total * D, transcendentals=total * n * FF),
        name="hidden",
    )(info, *xs, *weights)


def down_kernel(first, tile, info, h_line, h_near, h_other, h_last, own_w, wa, wb, o0, o1, o2, o3, w_buf, sem):
    width = w_buf.shape[1]
    wn = pl.multiple_of(info[3] * (FF // 2) + FF, FF // 2)
    wf = pl.multiple_of((1 - info[3]) * (FF // 2) + FF, FF // 2)
    copies = []
    for n in range(width // tile):
        cols = pl.ds(n * tile, tile)
        copies.append([
            pltpu.make_async_copy(own_w.at[:, pl.ds(first + n * tile, tile)], w_buf.at[pl.ds(0, FF), cols], sem.at[n, 0]),
            pltpu.make_async_copy(wa.at[:, cols], w_buf.at[pl.ds(wn, FF // 2), cols], sem.at[n, 1]),
            pltpu.make_async_copy(wb.at[:, cols], w_buf.at[pl.ds(wf, FF // 2), cols], sem.at[n, 2]),
        ])
        for c in copies[-1]:
            c.start()
    own = jnp.concatenate([h_line[...], h_near[...], h_last[:, :FF]], axis=0)
    other = jnp.concatenate([h_other[...], h_last[:, FF:]], axis=0)
    h = jnp.concatenate([own, other], axis=1)
    for n in range(width // tile):
        cols = pl.ds(n * tile, tile)
        for c in copies[n]:
            c.wait()
        y = jnp.dot(h, w_buf[:, cols], preferred_element_type=jnp.float32).astype(jnp.bfloat16)
        for i, o in enumerate((o0, o1, o2, o3)):
            o[:, cols] = y[i * LINE:(i + 1) * LINE]


def down(info, hs, first, own_w, wa, wb):
    hbm, vmem = pl.BlockSpec(memory_space=pltpu.HBM), pl.BlockSpec(memory_space=pltpu.VMEM)
    width = wa.shape[1]
    tile = 512
    total = 4 * LINE
    return pl.pallas_call(
        functools.partial(down_kernel, first, tile),
        out_shape=tuple(jax.ShapeDtypeStruct((LINE, width), jnp.bfloat16) for _ in range(4)),
        in_specs=[pl.BlockSpec(memory_space=pltpu.SMEM)] + [vmem] * len(hs) + [hbm] * 3,
        out_specs=(vmem,) * 4,
        scratch_shapes=[
            pltpu.VMEM((2 * FF, width), jnp.bfloat16),
            pltpu.SemaphoreType.DMA((width // tile, 3)),
        ],
        compiler_params=pltpu.CompilerParams(vmem_limit_bytes=24 * MIB),
        cost_estimate=pl.CostEstimate(flops=2 * total * 2 * FF * width, bytes_accessed=4 * FF * width + 2 * total * width, transcendentals=0),
        name="down",
    )(info, *hs, own_w, wa, wb)


def stack_kernel(*refs):
    at = 0
    for r in refs[:-1]:
        refs[-1][at:at + r.shape[0], :] = r[...]
        at += r.shape[0]


def stack(parts):
    vmem = pl.BlockSpec(memory_space=pltpu.VMEM)
    rows = sum(p.shape[0] for p in parts)
    return pl.pallas_call(
        stack_kernel,
        out_shape=jax.ShapeDtypeStruct((rows, D), jnp.bfloat16),
        in_specs=[vmem] * len(parts),
        out_specs=vmem,
        compiler_params=pltpu.CompilerParams(vmem_limit_bytes=16 * MIB),
        cost_estimate=pl.CostEstimate(flops=0, bytes_accessed=4 * rows * D, transcendentals=0),
        name="stack",
    )(*parts)


def combine_kernel(pick_ref, attn_ref, r0, r1, r2, r3, out_ref):
    for n in range(8):
        c = slice(n * 640, (n + 1) * 640)
        total = attn_ref[:, c].astype(jnp.float32)
        for i, r in enumerate((r0, r1, r2, r3)):
            total += lax.dot_general(
                pick_ref[i * 16:i * 16 + CAP], r[:, c], (((0,), (0,)), ((), ())), preferred_element_type=jnp.float32
            )
        out_ref[:, c] = total.astype(jnp.bfloat16)


def combine(pick, attn, rows):
    vmem = pl.BlockSpec(memory_space=pltpu.VMEM)
    return pl.pallas_call(
        combine_kernel,
        out_shape=jax.ShapeDtypeStruct((TOK, D), jnp.bfloat16),
        in_specs=[vmem] * 6,
        out_specs=vmem,
        compiler_params=pltpu.CompilerParams(vmem_limit_bytes=32 * MIB),
        cost_estimate=pl.CostEstimate(flops=60_000_000, bytes_accessed=3_000_000, transcendentals=0),
        name="combine",
    )(pick, attn, *rows)


def add_up(parts):
    total = parts[0].astype(jnp.float32)
    for p in parts[1:]:
        total = total + p.astype(jnp.float32)
    return total.astype(jnp.bfloat16)


def after(value, *others):
    return lax.optimization_barrier((value, others))[0]


def per_device(queries, key_rows, value_rows, segments, swap_flags, expert_ids, norm_gain, gate_weight, up_weight, down_weight):
    dp = lax.axis_index("dp")
    z = lax.axis_index("expert") // 16
    info = jnp.stack([swap_flags[0], z // 2, 1 - 2 * (z % 2), dp]).astype(jnp.int32)

    across = device_pairs(lambda d, zz, y, x: (d, zz ^ 1, y, x))
    beside = device_pairs(lambda d, zz, y, x: (1 - d, zz, y, x))
    g_first = send(lax.dynamic_slice_in_dim(gate_weight, dp * HALF, CUT, 0), across)

    seg_local = segments.astype(jnp.bfloat16)
    q1, k1, v1, s1 = (send(a, beside) for a in (queries, key_rows, value_rows, seg_local))
    seg = jnp.where(swap_flags[0] > 0, s1, seg_local)[0].astype(jnp.float32)
    position = jnp.arange(TOK)
    allowed = (seg[:, None] == seg[None, :]) & (position[:, None] >= position[None, :])
    bias = jnp.where(allowed, jnp.float32(0), jnp.float32(-1e30))
    attn, pick, *rows = attention(
        info, queries, q1, key_rows, k1, value_rows, v1, bias, expert_ids.reshape(1, TOK), norm_gain.reshape(1, D)
    )

    moved = [send(rows[k], to_expert(k)) for k in (1, 2, 3)]
    mine = jnp.concatenate([rows[0]] + after(moved, g_first), axis=0)
    g_rest = lax.dynamic_slice_in_dim(gate_weight, dp * HALF + CUT, HALF - CUT, 0)
    g_rest = send(after(g_rest, moved), across)
    line = stack([mine] + [send(mine, plane_shift(1, s)) for s in (1, 3, 2)])
    line_out = after(line, g_rest)
    c1, c3, c2 = (send(line_out, plane_shift(2, s)) for s in (1, 3, 2))
    u_half = lax.dynamic_slice_in_dim(up_weight, dp * HALF, HALF, 0)
    u_half = send(after(u_half, line_out), across)

    own_gu = (gate_weight, up_weight)
    h_line = hidden(info, [line], ("own",), own_gu)
    g_first, g_rest, u_half = after((g_first, g_rest, u_half), h_line)
    other_gu = (g_first, g_rest, send(g_first, beside), send(g_rest, beside), u_half, send(u_half, beside))
    h_near = hidden(info, [c1, c3], ("own",), own_gu, HINT)
    wa = []
    for col in (0, HALF):
        w = lax.dynamic_slice(down_weight, (dp * (FF // 2), col), (FF // 2, HALF))
        wa.append(send(after(w, line_out), across))
    h_other = hidden(info, [after(line, (h_near, wa[0])), c1, c3], ("other",), other_gu)
    wb0 = send(after(wa[0], h_near), beside)
    h_last = hidden(info, [after(c2, h_other)], ("own", "other"), own_gu + other_gu, 5 * HINT)
    hs = (h_line, h_near, h_other, h_last)

    def spread(outs, ahead):
        to = {True: 1, False: 3}
        relay = send(outs[3], plane_shift(2, to[ahead]))
        plain = send(outs[1 if ahead else 2], plane_shift(2, to[not ahead]))
        both = add_up([outs[2 if ahead else 1], relay])
        return [outs[0], plain, send(both, plane_shift(2, to[ahead]))], (plain, both)

    def line_sums(parts):
        back = [add_up([p[i * ROWS:(i + 1) * ROWS] for p in parts]) for i in range(4)]
        return [back[0]] + [send(b, plane_shift(1, s)) for b, s in zip(back[1:], (3, 1, 2))]

    outs0 = down(info, hs, 0, down_weight, wa[0], wb0)
    parts0, early = spread(outs0, True)
    hs = (h_line, h_near, h_other, after(h_last, early))
    wa[1] = after(wa[1], outs0[0])
    outs1 = down(info, hs, HALF, down_weight, wa[1], send(wa[1], beside))
    parts1, _ = spread(outs1, False)
    sums0 = line_sums(after(parts0, outs1[0]))
    sums1 = line_sums(parts1)
    mine_sum = jnp.concatenate([add_up(sums0), add_up(sums1)], axis=1)
    pieces = [mine_sum[k * CAP:(k + 1) * CAP] for k in range(4)]
    returned = [pieces[0]] + [send(pieces[k], reverse(to_expert(k))) for k in (1, 2, 3)]
    return combine(pick, attn, returned)


def solution(mesh):
    in_specs = (
        P(("dp", "expert"), None),
        P(("dp", "expert"), None),
        P(("dp", "expert"), None),
        P(("dp", "expert"), None),
        P("expert"),
        P(("dp", "expert"), None),
        P(),
        P(None, "expert"),
        P(None, "expert"),
        P("expert", None),
    )
    out_specs = P(("dp", "expert"), None)
    return jax.shard_map(
        per_device, mesh=mesh, in_specs=in_specs, out_specs=out_specs, check_vma=False
    )
```

```python
import functools
import itertools

import jax
import jax.numpy as jnp
from jax import lax
from jax.experimental import pallas as pl
from jax.experimental.pallas import tpu as pltpu
from jax.sharding import PartitionSpec as P

HEADS = 40
KVH = 8
GROUP = HEADS // KVH
HD = 128
D = 5120
FF = 256
EXP_WIN = 4
CAP = 10
TOK = 128
ROWS = EXP_WIN * CAP
LINE = 4 * ROWS
HALF = D // 2
CUT = 1280
ALL = ("dp", "expert")
MIB = 1 << 20
HINT = 6_000_000_000


def device_pairs(target):
    pairs = []
    for dp, z, y, x in itertools.product(range(2), range(8), range(4), range(4)):
        to = target(dp, z, y, x)
        pairs.append((((dp * 8 + z) * 4 + y) * 4 + x, ((to[0] * 8 + to[1]) * 4 + to[2]) * 4 + to[3]))
    return pairs


def plane_shift(phase, step):
    def target(dp, z, y, x):
        if (dp == 0) == (phase == 1):
            return dp, z, y, (x + step) % 4
        return dp, z, (y + step) % 4, x

    return device_pairs(target)


def to_expert(kind):
    offset = {1: (2, -2), 2: (-3, 3), 3: (-1, 1)}[kind]
    return device_pairs(lambda dp, z, y, x: (dp, (z + offset[z % 2]) % 8, y, x))


def reverse(pairs):
    return [(b, a) for a, b in pairs]


def send(value, pairs):
    return lax.ppermute(value, ALL, pairs)


def attention_kernel(info, q0, q1, k0, k1, v0, v1, bias_ref, route_ref, gain_ref, attn_ref, pick_ref, b0, b1, b2, b3, acc):
    moved = info[0] > 0
    bias = bias_ref[...]
    acc[...] = jnp.zeros_like(acc)
    for h in range(KVH):
        cols = slice(h * HD, (h + 1) * HD)
        key = jnp.where(moved, k1[:, cols], k0[:, cols])
        value = jnp.where(moved, v1[:, cols], v0[:, cols])
        heads = [slice((h * GROUP + g) * HD, (h * GROUP + g + 1) * HD) for g in range(GROUP)]
        query = jnp.concatenate([jnp.where(moved, q1[:, c], q0[:, c]) for c in heads], axis=0)
        scores = lax.dot_general(query, key, (((1,), (1,)), ((), ())), preferred_element_type=jnp.float32)
        scores = scores.reshape(GROUP, TOK, TOK) * HD ** (-0.5) + bias[None]
        top = jnp.max(scores, axis=-1, keepdims=True)
        expo = jnp.exp(scores - top)
        probs = (expo * (1.0 / jnp.sum(expo, axis=-1, keepdims=True))).astype(jnp.bfloat16)
        mixed = jnp.dot(probs.reshape(GROUP * TOK, TOK), value, preferred_element_type=jnp.float32)
        mixed = mixed.astype(jnp.bfloat16)
        for g, c in enumerate(heads):
            part = mixed[g * TOK:(g + 1) * TOK]
            attn_ref[:, c] = part
            part_f = part.astype(jnp.float32)
            acc[...] += part_f * part_f
    scale = lax.rsqrt(jnp.sum(acc[...], axis=-1, keepdims=True) * (1.0 / D) + 1e-05)
    route = route_ref[...]
    kind = jnp.where(route < EXP_WIN, ((route - info[1]) * info[2]) & 3, 64)
    lanes = lax.broadcasted_iota(jnp.int32, (TOK, TOK), 1)
    earlier = (lax.broadcasted_iota(jnp.int32, (TOK, TOK), 0) < lanes).astype(jnp.bfloat16)
    chosen = (lax.broadcasted_iota(jnp.int32, (16, TOK), 0) == kind).astype(jnp.bfloat16)
    order = jnp.dot(chosen, earlier, preferred_element_type=jnp.float32)
    slot = jnp.sum(chosen.astype(jnp.float32) * order, axis=0, keepdims=True).astype(jnp.int32)
    place = kind * 16 + slot
    pick = (lax.broadcasted_iota(jnp.int32, (64, TOK), 0) == place).astype(jnp.bfloat16)
    pick_ref[...] = pick
    for n in range(8):
        c = slice(n * 640, (n + 1) * 640)
        normed = (attn_ref[:, c].astype(jnp.float32) * scale * gain_ref[:, c].astype(jnp.float32)).astype(jnp.bfloat16)
        rows = jnp.dot(pick, normed, preferred_element_type=jnp.float32).astype(jnp.bfloat16)
        for i, b in enumerate((b0, b1, b2, b3)):
            b[:, c] = rows[i * 16:i * 16 + CAP]


def attention(info, q0, q1, k0, k1, v0, v1, bias, route, gain):
    vmem = pl.BlockSpec(memory_space=pltpu.VMEM)
    rows = jax.ShapeDtypeStruct((CAP, D), jnp.bfloat16)
    return pl.pallas_call(
        attention_kernel,
        out_shape=(
            jax.ShapeDtypeStruct((TOK, D), jnp.bfloat16),
            jax.ShapeDtypeStruct((64, TOK), jnp.bfloat16),
            rows, rows, rows, rows,
        ),
        in_specs=[pl.BlockSpec(memory_space=pltpu.SMEM)] + [vmem] * 9,
        out_specs=(vmem,) * 6,
        scratch_shapes=[pltpu.VMEM((TOK, TOK), jnp.float32)],
        compiler_params=pltpu.CompilerParams(vmem_limit_bytes=32 * MIB),
        cost_estimate=pl.CostEstimate(flops=400_000_000, bytes_accessed=6_000_000, transcendentals=660_000),
        name="attention",
    )(info, q0, q1, k0, k1, v0, v1, bias, route, gain)


def silu_mul(gate, up):
    return (gate / (1.0 + jnp.exp(-gate)) * up).astype(jnp.bfloat16)


def hidden_kernel(count, parts, info, *refs):
    xs, srcs, h_ref = refs[:count], list(refs[count:-1]), refs[-1]
    near = info[3] * HALF
    far = HALF - near
    for i, part in enumerate(parts):
        if part == "own":
            g, u = (srcs.pop(0) for _ in range(2))
            pieces = [(g.at[pl.ds(k, CUT)], u.at[pl.ds(k, CUT)], k) for k in range(0, D, CUT)]
        else:
            ga1, ga2, gb1, gb2, ua, ub = (srcs.pop(0) for _ in range(6))
            head, tail = pl.ds(0, CUT), pl.ds(CUT, CUT)
            pieces = [
                (ga1, ua.at[head], near),
                (ga2, ua.at[tail], near + CUT),
                (gb1, ub.at[head], far),
                (gb2, ub.at[tail], far + CUT),
            ]
        gate = up = None
        for g, u, k in pieces:
            at = pl.ds(k if isinstance(k, int) else pl.multiple_of(k, HD), CUT)
            x = jnp.concatenate([r[:, at] for r in xs], axis=0)
            gate_term = jnp.dot(x, g[...], preferred_element_type=jnp.float32)
            up_term = jnp.dot(x, u[...], preferred_element_type=jnp.float32)
            gate, up = (gate_term, up_term) if gate is None else (gate + gate_term, up + up_term)
        h_ref[:, i * FF:(i + 1) * FF] = silu_mul(gate, up)


def hidden(info, xs, parts, weights, flops=0):
    count, n = len(xs), len(parts)
    vmem = pl.BlockSpec(memory_space=pltpu.VMEM)
    total = count * LINE
    return pl.pallas_call(
        functools.partial(hidden_kernel, count, parts),
        out_shape=jax.ShapeDtypeStruct((total, n * FF), jnp.bfloat16),
        in_specs=[pl.BlockSpec(memory_space=pltpu.SMEM)] + [vmem] * (count + len(weights)),
        out_specs=vmem,
        compiler_params=pltpu.CompilerParams(vmem_limit_bytes=24 * MIB),
        cost_estimate=pl.CostEstimate(flops=max(flops, 4 * total * D * n * FF), bytes_accessed=4 * D * n * FF + 2 * total * D, transcendentals=total * n * FF),
        name="hidden",
    )(info, *xs, *weights)


def down_kernel(info, h_line, h_near, h_other, h_last, own_w, wa, wb, *outs):
    near = pl.ds(pl.multiple_of(info[3] * (FF // 2), FF // 2), FF // 2)
    far = pl.ds(pl.multiple_of((1 - info[3]) * (FF // 2), FF // 2), FF // 2)
    own = jnp.concatenate([h_line[...], h_near[...], h_last[:, :FF]], axis=0)
    last = h_last.at[:, pl.ds(FF, FF)]
    other = [jnp.concatenate([h_other[:, part], last[:, part]], axis=0) for part in (near, far)]
    h = jnp.concatenate([own, *other], axis=1)
    tile = 512
    for n in range(D // tile):
        cols = pl.ds(n * tile, tile)
        w = jnp.concatenate([own_w[:, cols], wa[:, cols], wb[:, cols]], axis=0)
        y = jnp.dot(h, w, preferred_element_type=jnp.float32).astype(jnp.bfloat16)
        half, at = divmod(n * tile, HALF)
        for i in range(4):
            outs[4 * half + i][:, at:at + tile] = y[i * LINE:(i + 1) * LINE]


def down(info, hs, own_w, wa, wb):
    vmem = pl.BlockSpec(memory_space=pltpu.VMEM)
    total = 4 * LINE
    outs = pl.pallas_call(
        down_kernel,
        out_shape=tuple(jax.ShapeDtypeStruct((LINE, HALF), jnp.bfloat16) for _ in range(8)),
        in_specs=[pl.BlockSpec(memory_space=pltpu.SMEM)] + [vmem] * (len(hs) + 3),
        out_specs=(vmem,) * 8,
        compiler_params=pltpu.CompilerParams(vmem_limit_bytes=24 * MIB),
        cost_estimate=pl.CostEstimate(flops=2 * total * 2 * FF * D, bytes_accessed=4 * FF * D + 2 * total * D, transcendentals=0),
        name="down",
    )(info, *hs, own_w, wa, wb)
    return outs[:4], outs[4:]


def hold(value, flops):
    hbm = pl.BlockSpec(memory_space=pl.ANY)
    return pl.pallas_call(
        lambda value_ref, out_ref: None,
        out_shape=jax.ShapeDtypeStruct(value.shape, value.dtype),
        in_specs=[hbm],
        out_specs=hbm,
        input_output_aliases={0: 0},
        cost_estimate=pl.CostEstimate(flops=flops, bytes_accessed=0, transcendentals=0),
        name="hold",
    )(value)


def line_sums_kernel(*refs):
    parts, outs = refs[:6], refs[6:]
    tile = 512
    for n in range(D // tile):
        half, at = divmod(n * tile, HALF)
        a, b, c = (r[:, at:at + tile].astype(jnp.float32) for r in parts[3 * half:3 * half + 3])
        total = a + b + c
        for i, o in enumerate(outs):
            o[:, n * tile:(n + 1) * tile] = total[i * ROWS:(i + 1) * ROWS].astype(jnp.bfloat16)


def line_sums(halves):
    vmem = pl.BlockSpec(memory_space=pltpu.VMEM)
    return pl.pallas_call(
        line_sums_kernel,
        out_shape=tuple(jax.ShapeDtypeStruct((ROWS, D), jnp.bfloat16) for _ in range(4)),
        in_specs=[vmem] * 6,
        out_specs=(vmem,) * 4,
        compiler_params=pltpu.CompilerParams(vmem_limit_bytes=24 * MIB),
        cost_estimate=pl.CostEstimate(flops=2 * LINE * D, bytes_accessed=8 * LINE * D, transcendentals=0),
        name="line_sums",
    )(*halves[0], *halves[1])


def stack_kernel(*refs):
    at = 0
    for r in refs[:-1]:
        refs[-1][at:at + r.shape[0], :] = r[...]
        at += r.shape[0]


def stack(parts):
    vmem = pl.BlockSpec(memory_space=pltpu.VMEM)
    rows = sum(p.shape[0] for p in parts)
    return pl.pallas_call(
        stack_kernel,
        out_shape=jax.ShapeDtypeStruct((rows, D), jnp.bfloat16),
        in_specs=[vmem] * len(parts),
        out_specs=vmem,
        compiler_params=pltpu.CompilerParams(vmem_limit_bytes=16 * MIB),
        cost_estimate=pl.CostEstimate(flops=0, bytes_accessed=4 * rows * D, transcendentals=0),
        name="stack",
    )(*parts)


def combine_kernel(pick_ref, attn_ref, r0, r1, r2, r3, out_ref):
    for n in range(8):
        c = slice(n * 640, (n + 1) * 640)
        total = attn_ref[:, c].astype(jnp.float32)
        for i, r in enumerate((r0, r1, r2, r3)):
            total += lax.dot_general(
                pick_ref[i * 16:i * 16 + CAP], r[:, c], (((0,), (0,)), ((), ())), preferred_element_type=jnp.float32
            )
        out_ref[:, c] = total.astype(jnp.bfloat16)


def combine(pick, attn, rows):
    vmem = pl.BlockSpec(memory_space=pltpu.VMEM)
    return pl.pallas_call(
        combine_kernel,
        out_shape=jax.ShapeDtypeStruct((TOK, D), jnp.bfloat16),
        in_specs=[vmem] * 6,
        out_specs=vmem,
        compiler_params=pltpu.CompilerParams(vmem_limit_bytes=32 * MIB),
        cost_estimate=pl.CostEstimate(flops=60_000_000, bytes_accessed=3_000_000, transcendentals=0),
        name="combine",
    )(pick, attn, *rows)


def add_up(parts):
    total = parts[0].astype(jnp.float32)
    for p in parts[1:]:
        total = total + p.astype(jnp.float32)
    return total.astype(jnp.bfloat16)


def after(value, *others):
    return lax.optimization_barrier((value, others))[0]


def per_device(queries, key_rows, value_rows, segments, swap_flags, expert_ids, norm_gain, gate_weight, up_weight, down_weight):
    dp = lax.axis_index("dp")
    z = lax.axis_index("expert") // 16
    info = jnp.stack([swap_flags[0], z // 2, 1 - 2 * (z % 2), dp]).astype(jnp.int32)

    across = device_pairs(lambda d, zz, y, x: (d, zz ^ 1, y, x))
    beside = device_pairs(lambda d, zz, y, x: (1 - d, zz, y, x))
    g_first = send(lax.dynamic_slice_in_dim(gate_weight, dp * HALF, CUT, 0), across)

    seg_local = segments.astype(jnp.bfloat16)
    q1, k1, v1, s1 = (send(a, beside) for a in (queries, key_rows, value_rows, seg_local))
    seg = jnp.where(swap_flags[0] > 0, s1, seg_local)[0].astype(jnp.float32)
    position = jnp.arange(TOK)
    allowed = (seg[:, None] == seg[None, :]) & (position[:, None] >= position[None, :])
    bias = jnp.where(allowed, jnp.float32(0), jnp.float32(-1e30))
    attn, pick, *rows = attention(
        info, queries, q1, key_rows, k1, value_rows, v1, bias, expert_ids.reshape(1, TOK), norm_gain.reshape(1, D)
    )

    moved = [send(rows[k], to_expert(k)) for k in (1, 2, 3)]
    mine = jnp.concatenate([rows[0]] + after(moved, g_first), axis=0)
    g_rest = lax.dynamic_slice_in_dim(gate_weight, dp * HALF + CUT, HALF - CUT, 0)
    g_rest = send(after(g_rest, moved), across)
    line = stack([mine] + [send(mine, plane_shift(1, s)) for s in (1, 3, 2)])
    line_out = after(line, g_rest)
    c1, c3, c2 = (send(line_out, plane_shift(2, s)) for s in (1, 3, 2))
    u_half = lax.dynamic_slice_in_dim(up_weight, dp * HALF, HALF, 0)
    u_half = send(after(u_half, line_out), across)

    own_gu = (gate_weight, up_weight)
    h_line = hidden(info, [line], ("own",), own_gu)
    g_first, g_rest, u_half = after((g_first, g_rest, u_half), h_line)
    other_gu = (g_first, g_rest, send(g_first, beside), send(g_rest, beside), u_half, send(u_half, beside))
    h_near = hidden(info, [c1, c3], ("own",), own_gu, HINT)
    wa = send(after(lax.dynamic_slice_in_dim(down_weight, dp * (FF // 2), FF // 2, 0), line_out), across)
    h_other = hidden(info, [after(line, h_near), c1, c3], ("other",), other_gu)
    h_last = hidden(info, [after(c2, h_other)], ("own", "other"), own_gu + other_gu)
    hs = (h_line, h_near, h_other, h_last)

    wa = after(wa, h_last)
    outs0, outs1 = down(info, hs, down_weight, wa, send(wa, beside))

    relay0 = send(outs0[3], plane_shift(2, 1))
    relay1 = send(outs1[3], plane_shift(2, 3))
    plain0 = send(outs0[1], plane_shift(2, 3))
    plain1 = send(outs1[2], plane_shift(2, 1))
    both0 = send(add_up([outs0[2], relay0]), plane_shift(2, 1))
    both1 = send(add_up([outs1[1], relay1]), plane_shift(2, 3))
    halves = ((outs0[0], plain0, both0), (outs1[0], plain1, both1))
    back = line_sums(halves)
    mine_sum = add_up([back[0]] + [send(b, plane_shift(1, s)) for b, s in zip(back[1:], (3, 1, 2))])
    pieces = [mine_sum[k * CAP:(k + 1) * CAP] for k in range(4)]
    returned = [pieces[0]] + [send(pieces[k], reverse(to_expert(k))) for k in (1, 2, 3)]
    return combine(pick, attn, returned)


def solution(mesh):
    in_specs = (
        P(("dp", "expert"), None),
        P(("dp", "expert"), None),
        P(("dp", "expert"), None),
        P(("dp", "expert"), None),
        P("expert"),
        P(("dp", "expert"), None),
        P(),
        P(None, "expert"),
        P(None, "expert"),
        P("expert", None),
    )
    out_specs = P(("dp", "expert"), None)
    return jax.shard_map(
        per_device, mesh=mesh, in_specs=in_specs, out_specs=out_specs, check_vma=False
    )
```

```python
import functools
import itertools

import jax
import jax.numpy as jnp
from jax import lax
from jax.experimental import pallas as pl
from jax.experimental.pallas import tpu as pltpu
from jax.sharding import PartitionSpec as P

HEADS = 40
KVH = 8
GROUP = HEADS // KVH
HD = 128
D = 5120
FF = 256
EXP_WIN = 4
CAP = 10
TOK = 128
ROWS = EXP_WIN * CAP
LINE = 4 * ROWS
HALF = D // 2
CUT = 1280
ALL = ("dp", "expert")
MIB = 1 << 20
HINT = 6_000_000_000


def device_pairs(target):
    pairs = []
    for dp, z, y, x in itertools.product(range(2), range(8), range(4), range(4)):
        to = target(dp, z, y, x)
        pairs.append((((dp * 8 + z) * 4 + y) * 4 + x, ((to[0] * 8 + to[1]) * 4 + to[2]) * 4 + to[3]))
    return pairs


def plane_shift(phase, step):
    def target(dp, z, y, x):
        if (dp == 0) == (phase == 1):
            return dp, z, y, (x + step) % 4
        return dp, z, (y + step) % 4, x

    return device_pairs(target)


def to_expert(kind):
    offset = {1: (2, -2), 2: (-3, 3), 3: (-1, 1)}[kind]
    return device_pairs(lambda dp, z, y, x: (dp, (z + offset[z % 2]) % 8, y, x))


def reverse(pairs):
    return [(b, a) for a, b in pairs]


def send(value, pairs):
    return lax.ppermute(value, ALL, pairs)


def attention_kernel(info, q0, q1, k0, k1, v0, v1, bias_ref, route_ref, gain_ref, attn_ref, pick_ref, b0, b1, b2, b3, acc):
    moved = info[0] > 0
    bias = bias_ref[...]
    acc[...] = jnp.zeros_like(acc)
    for h in range(KVH):
        cols = slice(h * HD, (h + 1) * HD)
        key = jnp.where(moved, k1[:, cols], k0[:, cols])
        value = jnp.where(moved, v1[:, cols], v0[:, cols])
        heads = [slice((h * GROUP + g) * HD, (h * GROUP + g + 1) * HD) for g in range(GROUP)]
        query = jnp.concatenate([jnp.where(moved, q1[:, c], q0[:, c]) for c in heads], axis=0)
        scores = lax.dot_general(query, key, (((1,), (1,)), ((), ())), preferred_element_type=jnp.float32)
        scores = scores.reshape(GROUP, TOK, TOK) * HD ** (-0.5) + bias[None]
        top = jnp.max(scores, axis=-1, keepdims=True)
        expo = jnp.exp(scores - top)
        probs = (expo * (1.0 / jnp.sum(expo, axis=-1, keepdims=True))).astype(jnp.bfloat16)
        mixed = jnp.dot(probs.reshape(GROUP * TOK, TOK), value, preferred_element_type=jnp.float32)
        mixed = mixed.astype(jnp.bfloat16)
        for g, c in enumerate(heads):
            part = mixed[g * TOK:(g + 1) * TOK]
            attn_ref[:, c] = part
            part_f = part.astype(jnp.float32)
            acc[...] += part_f * part_f
    scale = lax.rsqrt(jnp.sum(acc[...], axis=-1, keepdims=True) * (1.0 / D) + 1e-05)
    route = route_ref[...]
    kind = jnp.where(route < EXP_WIN, ((route - info[1]) * info[2]) & 3, 64)
    lanes = lax.broadcasted_iota(jnp.int32, (TOK, TOK), 1)
    earlier = (lax.broadcasted_iota(jnp.int32, (TOK, TOK), 0) < lanes).astype(jnp.bfloat16)
    chosen = (lax.broadcasted_iota(jnp.int32, (16, TOK), 0) == kind).astype(jnp.bfloat16)
    order = jnp.dot(chosen, earlier, preferred_element_type=jnp.float32)
    slot = jnp.sum(chosen.astype(jnp.float32) * order, axis=0, keepdims=True).astype(jnp.int32)
    place = kind * 16 + slot
    pick = (lax.broadcasted_iota(jnp.int32, (64, TOK), 0) == place).astype(jnp.bfloat16)
    pick_ref[...] = pick
    for n in range(8):
        c = slice(n * 640, (n + 1) * 640)
        normed = (attn_ref[:, c].astype(jnp.float32) * scale * gain_ref[:, c].astype(jnp.float32)).astype(jnp.bfloat16)
        rows = jnp.dot(pick, normed, preferred_element_type=jnp.float32).astype(jnp.bfloat16)
        for i, b in enumerate((b0, b1, b2, b3)):
            b[:, c] = rows[i * 16:i * 16 + CAP]


def attention(info, q0, q1, k0, k1, v0, v1, bias, route, gain):
    vmem = pl.BlockSpec(memory_space=pltpu.VMEM)
    rows = jax.ShapeDtypeStruct((CAP, D), jnp.bfloat16)
    return pl.pallas_call(
        attention_kernel,
        out_shape=(
            jax.ShapeDtypeStruct((TOK, D), jnp.bfloat16),
            jax.ShapeDtypeStruct((64, TOK), jnp.bfloat16),
            rows, rows, rows, rows,
        ),
        in_specs=[pl.BlockSpec(memory_space=pltpu.SMEM)] + [vmem] * 9,
        out_specs=(vmem,) * 6,
        scratch_shapes=[pltpu.VMEM((TOK, TOK), jnp.float32)],
        compiler_params=pltpu.CompilerParams(vmem_limit_bytes=14 * MIB),
        cost_estimate=pl.CostEstimate(flops=400_000_000, bytes_accessed=6_000_000, transcendentals=660_000),
        name="attention",
    )(info, q0, q1, k0, k1, v0, v1, bias, route, gain)


def silu_mul(gate, up):
    return (gate / (1.0 + jnp.exp(-gate)) * up).astype(jnp.bfloat16)


def hidden_kernel(count, parts, info, *refs):
    xs, srcs, h_ref = refs[:count], list(refs[count:-1]), refs[-1]
    near = info[3] * HALF
    far = HALF - near
    for i, part in enumerate(parts):
        if part == "own":
            g, u = (srcs.pop(0) for _ in range(2))
            pieces = [(g.at[pl.ds(k, CUT)], u.at[pl.ds(k, CUT)], k) for k in range(0, D, CUT)]
        else:
            ga1, ga2, gb1, gb2, ua, ub = (srcs.pop(0) for _ in range(6))
            head, tail = pl.ds(0, CUT), pl.ds(CUT, CUT)
            pieces = [
                (ga1, ua.at[head], near),
                (ga2, ua.at[tail], near + CUT),
                (gb1, ub.at[head], far),
                (gb2, ub.at[tail], far + CUT),
            ]
        gate = up = None
        for g, u, k in pieces:
            at = pl.ds(k if isinstance(k, int) else pl.multiple_of(k, HD), CUT)
            x = jnp.concatenate([r[:, at] for r in xs], axis=0)
            gate_term = jnp.dot(x, g[...], preferred_element_type=jnp.float32)
            up_term = jnp.dot(x, u[...], preferred_element_type=jnp.float32)
            gate, up = (gate_term, up_term) if gate is None else (gate + gate_term, up + up_term)
        h_ref[:, i * FF:(i + 1) * FF] = silu_mul(gate, up)


def hidden(info, xs, parts, weights, flops=0):
    count, n = len(xs), len(parts)
    vmem = pl.BlockSpec(memory_space=pltpu.VMEM)
    total = count * LINE
    return pl.pallas_call(
        functools.partial(hidden_kernel, count, parts),
        out_shape=jax.ShapeDtypeStruct((total, n * FF), jnp.bfloat16),
        in_specs=[pl.BlockSpec(memory_space=pltpu.SMEM)] + [vmem] * (count + len(weights)),
        out_specs=vmem,
        compiler_params=pltpu.CompilerParams(vmem_limit_bytes=18 * MIB),
        cost_estimate=pl.CostEstimate(flops=max(flops, 4 * total * D * n * FF), bytes_accessed=4 * D * n * FF + 2 * total * D, transcendentals=total * n * FF),
        name="hidden",
    )(info, *xs, *weights)


def down_kernel(info, h_line, h_near, h_other, h_last, own_w, wa, wb, *outs):
    near = pl.ds(pl.multiple_of(info[3] * (FF // 2), FF // 2), FF // 2)
    far = pl.ds(pl.multiple_of((1 - info[3]) * (FF // 2), FF // 2), FF // 2)
    own = jnp.concatenate([h_line[...], h_near[...], h_last[:, :FF]], axis=0)
    last = h_last.at[:, pl.ds(FF, FF)]
    other = [jnp.concatenate([h_other[:, part], last[:, part]], axis=0) for part in (near, far)]
    h = jnp.concatenate([own, *other], axis=1)
    tile = 512
    for n in range(D // tile):
        cols = pl.ds(n * tile, tile)
        w = jnp.concatenate([own_w[:, cols], wa[:, cols], wb[:, cols]], axis=0)
        y = jnp.dot(h, w, preferred_element_type=jnp.float32).astype(jnp.bfloat16)
        half, at = divmod(n * tile, HALF)
        for i in range(4):
            outs[4 * half + i][:, at:at + tile] = y[i * LINE:(i + 1) * LINE]


def down(info, hs, own_w, wa, wb):
    vmem = pl.BlockSpec(memory_space=pltpu.VMEM)
    total = 4 * LINE
    outs = pl.pallas_call(
        down_kernel,
        out_shape=tuple(jax.ShapeDtypeStruct((LINE, HALF), jnp.bfloat16) for _ in range(8)),
        in_specs=[pl.BlockSpec(memory_space=pltpu.SMEM)] + [vmem] * (len(hs) + 3),
        out_specs=(vmem,) * 8,
        compiler_params=pltpu.CompilerParams(vmem_limit_bytes=20 * MIB),
        cost_estimate=pl.CostEstimate(flops=2 * total * 2 * FF * D, bytes_accessed=4 * FF * D + 2 * total * D, transcendentals=0),
        name="down",
    )(info, *hs, own_w, wa, wb)
    return outs[:4], outs[4:]


def hold(value, flops):
    hbm = pl.BlockSpec(memory_space=pl.ANY)
    return pl.pallas_call(
        lambda value_ref, out_ref: None,
        out_shape=jax.ShapeDtypeStruct(value.shape, value.dtype),
        in_specs=[hbm],
        out_specs=hbm,
        input_output_aliases={0: 0},
        compiler_params=pltpu.CompilerParams(vmem_limit_bytes=MIB),
        cost_estimate=pl.CostEstimate(flops=flops, bytes_accessed=0, transcendentals=0),
        name="hold",
    )(value)


def line_sums_kernel(*refs):
    parts, outs = refs[:6], refs[6:]
    tile = 512
    for n in range(D // tile):
        half, at = divmod(n * tile, HALF)
        a, b, c = (r[:, at:at + tile].astype(jnp.float32) for r in parts[3 * half:3 * half + 3])
        total = a + b + c
        for i, o in enumerate(outs):
            o[:, n * tile:(n + 1) * tile] = total[i * ROWS:(i + 1) * ROWS].astype(jnp.bfloat16)


def line_sums(halves):
    vmem = pl.BlockSpec(memory_space=pltpu.VMEM)
    return pl.pallas_call(
        line_sums_kernel,
        out_shape=tuple(jax.ShapeDtypeStruct((ROWS, D), jnp.bfloat16) for _ in range(4)),
        in_specs=[vmem] * 6,
        out_specs=(vmem,) * 4,
        compiler_params=pltpu.CompilerParams(vmem_limit_bytes=12 * MIB),
        cost_estimate=pl.CostEstimate(flops=2 * LINE * D, bytes_accessed=8 * LINE * D, transcendentals=0),
        name="line_sums",
    )(*halves[0], *halves[1])


def stack_kernel(*refs):
    at = 0
    for r in refs[:-1]:
        refs[-1][at:at + r.shape[0], :] = r[...]
        at += r.shape[0]


def stack(parts):
    vmem = pl.BlockSpec(memory_space=pltpu.VMEM)
    rows = sum(p.shape[0] for p in parts)
    return pl.pallas_call(
        stack_kernel,
        out_shape=jax.ShapeDtypeStruct((rows, D), jnp.bfloat16),
        in_specs=[vmem] * len(parts),
        out_specs=vmem,
        compiler_params=pltpu.CompilerParams(vmem_limit_bytes=8 * MIB),
        cost_estimate=pl.CostEstimate(flops=0, bytes_accessed=4 * rows * D, transcendentals=0),
        name="stack",
    )(*parts)


def combine_kernel(pick_ref, attn_ref, r0, r1, r2, r3, out_ref):
    for n in range(8):
        c = slice(n * 640, (n + 1) * 640)
        total = attn_ref[:, c].astype(jnp.float32)
        for i, r in enumerate((r0, r1, r2, r3)):
            total += lax.dot_general(
                pick_ref[i * 16:i * 16 + CAP], r[:, c], (((0,), (0,)), ((), ())), preferred_element_type=jnp.float32
            )
        out_ref[:, c] = total.astype(jnp.bfloat16)


def combine(pick, attn, rows):
    vmem = pl.BlockSpec(memory_space=pltpu.VMEM)
    return pl.pallas_call(
        combine_kernel,
        out_shape=jax.ShapeDtypeStruct((TOK, D), jnp.bfloat16),
        in_specs=[vmem] * 6,
        out_specs=vmem,
        compiler_params=pltpu.CompilerParams(vmem_limit_bytes=10 * MIB),
        cost_estimate=pl.CostEstimate(flops=60_000_000, bytes_accessed=3_000_000, transcendentals=0),
        name="combine",
    )(pick, attn, *rows)


def add_up(parts):
    total = parts[0].astype(jnp.float32)
    for p in parts[1:]:
        total = total + p.astype(jnp.float32)
    return total.astype(jnp.bfloat16)


def after(value, *others):
    return lax.optimization_barrier((value, others))[0]


def per_device(queries, key_rows, value_rows, segments, swap_flags, expert_ids, norm_gain, gate_weight, up_weight, down_weight):
    dp = lax.axis_index("dp")
    z = lax.axis_index("expert") // 16
    info = jnp.stack([swap_flags[0], z // 2, 1 - 2 * (z % 2), dp]).astype(jnp.int32)

    across = device_pairs(lambda d, zz, y, x: (d, zz ^ 1, y, x))
    beside = device_pairs(lambda d, zz, y, x: (1 - d, zz, y, x))
    g_first = send(lax.dynamic_slice_in_dim(gate_weight, dp * HALF, CUT, 0), across)

    seg_local = segments.astype(jnp.bfloat16)
    q1, k1, v1, s1 = (send(a, beside) for a in (queries, key_rows, value_rows, seg_local))
    seg = jnp.where(swap_flags[0] > 0, s1, seg_local)[0].astype(jnp.float32)
    position = jnp.arange(TOK)
    allowed = (seg[:, None] == seg[None, :]) & (position[:, None] >= position[None, :])
    bias = jnp.where(allowed, jnp.float32(0), jnp.float32(-1e30))
    attn, pick, *rows = attention(
        info, queries, q1, key_rows, k1, value_rows, v1, bias, expert_ids.reshape(1, TOK), norm_gain.reshape(1, D)
    )

    moved = [send(rows[k], to_expert(k)) for k in (1, 2, 3)]
    mine = jnp.concatenate([rows[0]] + after(moved, g_first), axis=0)
    g_rest = lax.dynamic_slice_in_dim(gate_weight, dp * HALF + CUT, HALF - CUT, 0)
    g_rest = send(after(g_rest, pick), across)
    line = stack([mine] + [send(mine, plane_shift(1, s)) for s in (1, 3, 2)])
    c1, c3, c2 = (send(line, plane_shift(2, s)) for s in (1, 3, 2))
    u_half = lax.dynamic_slice_in_dim(up_weight, dp * HALF, HALF, 0)
    u_half = send(after(u_half, moved), across)

    own_gu = (gate_weight, up_weight)
    g_rest = hold(g_rest, 3*HINT)
    h_line = hidden(info, [after(line, g_rest)], ("own",), own_gu)
    g_first, g_rest, u_half = after((g_first, g_rest, u_half), h_line)
    other_gu = (g_first, g_rest, send(g_first, beside), send(g_rest, beside), u_half, send(u_half, beside))
    h_near = hidden(info, [c1, c3], ("own",), own_gu, HINT)
    wa = send(after(lax.dynamic_slice_in_dim(down_weight, dp * (FF // 2), FF // 2, 0), line), across)
    h_other = hidden(info, [after(line, h_near), c1, c3], ("other",), other_gu)
    wa = hold(after(wa, (h_other, c2)), 3*HINT//2)
    h_last = hidden(info, [after(c2, wa)], ("own", "other"), own_gu + other_gu)
    hs = (h_line, h_near, h_other, h_last)

    outs0, outs1 = down(info, hs, down_weight, wa, send(wa, beside))

    relay0 = send(outs0[3], plane_shift(2, 1))
    relay1 = send(outs1[3], plane_shift(2, 3))
    plain0 = send(outs0[1], plane_shift(2, 3))
    plain1 = send(outs1[2], plane_shift(2, 1))
    both0 = send(add_up([outs0[2], relay0]), plane_shift(2, 1))
    both1 = send(add_up([outs1[1], relay1]), plane_shift(2, 3))
    halves = ((outs0[0], plain0, both0), (outs1[0], plain1, both1))
    back = line_sums(halves)
    mine_sum = add_up([back[0]] + [send(b, plane_shift(1, s)) for b, s in zip(back[1:], (3, 1, 2))])
    pieces = [mine_sum[k * CAP:(k + 1) * CAP] for k in range(4)]
    returned = [pieces[0]] + [send(pieces[k], reverse(to_expert(k))) for k in (1, 2, 3)]
    return combine(pick, attn, returned)


def solution(mesh):
    in_specs = (
        P(("dp", "expert"), None),
        P(("dp", "expert"), None),
        P(("dp", "expert"), None),
        P(("dp", "expert"), None),
        P("expert"),
        P(("dp", "expert"), None),
        P(),
        P(None, "expert"),
        P(None, "expert"),
        P("expert", None),
    )
    out_specs = P(("dp", "expert"), None)
    return jax.shard_map(
        per_device, mesh=mesh, in_specs=in_specs, out_specs=out_specs, check_vma=False
    )
```

```python
import functools
import itertools

import jax
import jax.numpy as jnp
from jax import lax
from jax.experimental import pallas as pl
from jax.experimental.pallas import tpu as pltpu
from jax.sharding import PartitionSpec as P

HEADS = 40
KVH = 8
GROUP = HEADS // KVH
HD = 128
D = 5120
FF = 256
EXP_WIN = 4
CAP = 10
TOK = 128
ROWS = EXP_WIN * CAP
LINE = 4 * ROWS
HALF = D // 2
QUARTER = D // 4
CUT = 1280
ALL = ("dp", "expert")
MIB = 1 << 20
HINT = 6_000_000_000


def device_pairs(target):
    pairs = []
    for dp, z, y, x in itertools.product(range(2), range(8), range(4), range(4)):
        to = target(dp, z, y, x)
        pairs.append((((dp * 8 + z) * 4 + y) * 4 + x, ((to[0] * 8 + to[1]) * 4 + to[2]) * 4 + to[3]))
    return pairs


def plane_shift(phase, step):
    def target(dp, z, y, x):
        if (dp == 0) == (phase == 1):
            return dp, z, y, (x + step) % 4
        return dp, z, (y + step) % 4, x

    return device_pairs(target)


def to_expert(kind):
    offset = {1: (2, -2), 2: (-3, 3), 3: (-1, 1)}[kind]
    return device_pairs(lambda dp, z, y, x: (dp, (z + offset[z % 2]) % 8, y, x))


def reverse(pairs):
    return [(b, a) for a, b in pairs]


def send(value, pairs):
    return lax.ppermute(value, ALL, pairs)


def attention_kernel(info, q0, q1, k0, k1, v0, v1, bias_ref, route_ref, gain_ref, attn_ref, code_ref, b0, b1, b2, b3, acc, q, k, v, sem):
    kept = [pltpu.make_async_copy(a, b, sem.at[i]) for i, (a, b) in enumerate(((k0, k), (q0, q), (v0, v)))]
    swapped = [pltpu.make_async_copy(a, b, sem.at[i]) for i, (a, b) in enumerate(((k1, k), (q1, q), (v1, v)))]

    @pl.when(info[0] > 0)
    def _():
        for c in swapped:
            c.start()

    @pl.when(info[0] <= 0)
    def _():
        for c in kept:
            c.start()

    bias = bias_ref[...]
    acc[...] = jnp.zeros_like(acc)
    for c in kept:
        c.wait()
    for h in range(KVH):
        cols = slice(h * HD, (h + 1) * HD)
        key = k[:, cols]
        value = v[:, cols]
        heads = [slice((h * GROUP + g) * HD, (h * GROUP + g + 1) * HD) for g in range(GROUP)]
        query = jnp.concatenate([q[:, c] for c in heads], axis=0)
        scores = lax.dot_general(query, key, (((1,), (1,)), ((), ())), preferred_element_type=jnp.float32)
        scores = scores.reshape(GROUP, TOK, TOK) * HD ** (-0.5) + bias[None]
        top = jnp.max(scores, axis=-1, keepdims=True)
        expo = jnp.exp(scores - top)
        probs = (expo * (1.0 / jnp.sum(expo, axis=-1, keepdims=True))).astype(jnp.bfloat16)
        mixed = jnp.dot(probs.reshape(GROUP * TOK, TOK), value, preferred_element_type=jnp.float32)
        mixed = mixed.astype(jnp.bfloat16)
        for g, c in enumerate(heads):
            part = mixed[g * TOK:(g + 1) * TOK]
            attn_ref[:, c] = part
            part_f = part.astype(jnp.float32)
            acc[...] += part_f * part_f
    scale = lax.rsqrt(jnp.sum(acc[...], axis=-1, keepdims=True) * (1.0 / D) + 1e-05)
    route = route_ref[...]
    kind = jnp.where(route < EXP_WIN, ((route - info[1]) * info[2]) & 3, 64)
    lanes = lax.broadcasted_iota(jnp.int32, (TOK, TOK), 1)
    earlier = (lax.broadcasted_iota(jnp.int32, (TOK, TOK), 0) < lanes).astype(jnp.bfloat16)
    chosen = (lax.broadcasted_iota(jnp.int32, (16, TOK), 0) == kind).astype(jnp.bfloat16)
    order = jnp.dot(chosen, earlier, preferred_element_type=jnp.float32)
    slot = jnp.sum(chosen.astype(jnp.float32) * order, axis=0, keepdims=True).astype(jnp.int32)
    code = jnp.where(kind < EXP_WIN, kind * ROWS + slot, -1000)
    code_ref[...] = code
    rows_at = lax.broadcasted_iota(jnp.int32, (4 * ROWS, TOK), 0)
    picks = [(rows_at == code + q * CAP).astype(jnp.bfloat16) for q in range(4)]
    half = QUARTER // 2
    for n in range(2):
        rows = None
        for q in range(4):
            c = slice(q * QUARTER + n * half, q * QUARTER + (n + 1) * half)
            normed = (attn_ref[:, c].astype(jnp.float32) * scale * gain_ref[:, c].astype(jnp.float32)).astype(jnp.bfloat16)
            term = jnp.dot(picks[q], normed, preferred_element_type=jnp.float32)
            rows = term if rows is None else rows + term
        for i, b in enumerate((b0, b1, b2, b3)):
            b[:, n * half:(n + 1) * half] = rows[i * ROWS:(i + 1) * ROWS].astype(jnp.bfloat16)


def attention(info, q0, q1, k0, k1, v0, v1, bias, route, gain):
    vmem = pl.BlockSpec(memory_space=pltpu.VMEM)
    rows = jax.ShapeDtypeStruct((ROWS, QUARTER), jnp.bfloat16)
    return pl.pallas_call(
        attention_kernel,
        out_shape=(
            jax.ShapeDtypeStruct((TOK, D), jnp.bfloat16),
            jax.ShapeDtypeStruct((1, TOK), jnp.int32),
            rows, rows, rows, rows,
        ),
        in_specs=[pl.BlockSpec(memory_space=pltpu.SMEM)] + [pl.BlockSpec(memory_space=pl.ANY)] * 6 + [vmem] * 3,
        out_specs=(vmem,) * 6,
        scratch_shapes=[
            pltpu.VMEM((TOK, TOK), jnp.float32),
            pltpu.VMEM((TOK, D), jnp.bfloat16),
            pltpu.VMEM((TOK, KVH * HD), jnp.bfloat16),
            pltpu.VMEM((TOK, KVH * HD), jnp.bfloat16),
            pltpu.SemaphoreType.DMA((3,)),
        ],
        compiler_params=pltpu.CompilerParams(vmem_limit_bytes=56 * MIB),
        cost_estimate=pl.CostEstimate(flops=400_000_000, bytes_accessed=6_000_000, transcendentals=660_000),
        name="attention",
    )(info, q0, q1, k0, k1, v0, v1, bias, route, gain)


def silu_mul(gate, up):
    return (gate / (1.0 + jnp.exp(-gate)) * up).astype(jnp.bfloat16)


def hidden_kernel(count, parts, info, *refs):
    xs, srcs, h_ref = refs[:count], list(refs[count:-1]), refs[-1]
    near = info[3] * HALF
    far = HALF - near
    for i, part in enumerate(parts):
        if part == "own":
            g, u = (srcs.pop(0) for _ in range(2))
            pieces = [(g.at[pl.ds(k, CUT)], u.at[pl.ds(k, CUT)], k) for k in range(0, D, CUT)]
        else:
            ga1, ga2, gb1, gb2, ua, ub = (srcs.pop(0) for _ in range(6))
            head, tail = pl.ds(0, CUT), pl.ds(CUT, CUT)
            pieces = [
                (ga1, ua.at[head], near),
                (ga2, ua.at[tail], near + CUT),
                (gb1, ub.at[head], far),
                (gb2, ub.at[tail], far + CUT),
            ]
        gate = up = None
        for g, u, k in pieces:
            at = pl.ds(k if isinstance(k, int) else pl.multiple_of(k, HD), CUT)
            x = jnp.concatenate([r[:, at] for r in xs], axis=0)
            gate_term = jnp.dot(x, g[...], preferred_element_type=jnp.float32)
            up_term = jnp.dot(x, u[...], preferred_element_type=jnp.float32)
            gate, up = (gate_term, up_term) if gate is None else (gate + gate_term, up + up_term)
        h_ref[:, i * FF:(i + 1) * FF] = silu_mul(gate, up)


def hidden(info, xs, parts, weights, flops=0):
    count, n = len(xs), len(parts)
    vmem = pl.BlockSpec(memory_space=pltpu.VMEM)
    total = count * LINE
    return pl.pallas_call(
        functools.partial(hidden_kernel, count, parts),
        out_shape=jax.ShapeDtypeStruct((total, n * FF), jnp.bfloat16),
        in_specs=[pl.BlockSpec(memory_space=pltpu.SMEM)] + [vmem] * (count + len(weights)),
        out_specs=vmem,
        compiler_params=pltpu.CompilerParams(vmem_limit_bytes=18 * MIB),
        cost_estimate=pl.CostEstimate(flops=max(flops, 4 * total * D * n * FF), bytes_accessed=4 * D * n * FF + 2 * total * D, transcendentals=total * n * FF),
        name="hidden",
    )(info, *xs, *weights)


def down_kernel(info, h_line, h_near, h_other, h_last, own_w, wa, wb, *outs):
    near = pl.ds(pl.multiple_of(info[3] * (FF // 2), FF // 2), FF // 2)
    far = pl.ds(pl.multiple_of((1 - info[3]) * (FF // 2), FF // 2), FF // 2)
    own = jnp.concatenate([h_line[...], h_near[...], h_last[:, :FF]], axis=0)
    last = h_last.at[:, pl.ds(FF, FF)]
    other = [jnp.concatenate([h_other[:, part], last[:, part]], axis=0) for part in (near, far)]
    h = jnp.concatenate([own, *other], axis=1)
    tile = 512
    for n in range(D // tile):
        cols = pl.ds(n * tile, tile)
        w = jnp.concatenate([own_w[:, cols], wa[:, cols], wb[:, cols]], axis=0)
        y = jnp.dot(h, w, preferred_element_type=jnp.float32).astype(jnp.bfloat16)
        half, at = divmod(n * tile, HALF)
        for i in range(4):
            outs[4 * half + i][:, at:at + tile] = y[i * LINE:(i + 1) * LINE]


def down(info, hs, own_w, wa, wb):
    vmem = pl.BlockSpec(memory_space=pltpu.VMEM)
    total = 4 * LINE
    outs = pl.pallas_call(
        down_kernel,
        out_shape=tuple(jax.ShapeDtypeStruct((LINE, HALF), jnp.bfloat16) for _ in range(8)),
        in_specs=[pl.BlockSpec(memory_space=pltpu.SMEM)] + [vmem] * (len(hs) + 3),
        out_specs=(vmem,) * 8,
        compiler_params=pltpu.CompilerParams(vmem_limit_bytes=20 * MIB),
        cost_estimate=pl.CostEstimate(flops=2 * total * 2 * FF * D, bytes_accessed=4 * FF * D + 2 * total * D, transcendentals=0),
        name="down",
    )(info, *hs, own_w, wa, wb)
    return outs[:4], outs[4:]


def hold(value, flops):
    hbm = pl.BlockSpec(memory_space=pl.ANY)
    return pl.pallas_call(
        lambda value_ref, out_ref: None,
        out_shape=jax.ShapeDtypeStruct(value.shape, value.dtype),
        in_specs=[hbm],
        out_specs=hbm,
        input_output_aliases={0: 0},
        compiler_params=pltpu.CompilerParams(vmem_limit_bytes=MIB),
        cost_estimate=pl.CostEstimate(flops=flops, bytes_accessed=0, transcendentals=0),
        name="hold",
    )(value)


def line_sums_kernel(*refs):
    parts, outs = refs[:6], refs[6:]
    tile = 512
    for n in range(D // tile):
        half, at = divmod(n * tile, HALF)
        a, b, c = (r[:, at:at + tile].astype(jnp.float32) for r in parts[3 * half:3 * half + 3])
        total = a + b + c
        for i, o in enumerate(outs):
            o[:, n * tile:(n + 1) * tile] = total[i * ROWS:(i + 1) * ROWS].astype(jnp.bfloat16)


def line_sums(halves):
    vmem = pl.BlockSpec(memory_space=pltpu.VMEM)
    return pl.pallas_call(
        line_sums_kernel,
        out_shape=tuple(jax.ShapeDtypeStruct((ROWS, D), jnp.bfloat16) for _ in range(4)),
        in_specs=[vmem] * 6,
        out_specs=(vmem,) * 4,
        compiler_params=pltpu.CompilerParams(vmem_limit_bytes=12 * MIB),
        cost_estimate=pl.CostEstimate(flops=2 * LINE * D, bytes_accessed=8 * LINE * D, transcendentals=0),
        name="line_sums",
    )(*halves[0], *halves[1])


def stack_kernel(*refs):
    at = 0
    for r in refs[:-1]:
        refs[-1][at:at + r.shape[0], :] = r[...]
        at += r.shape[0]


def stack(parts):
    vmem = pl.BlockSpec(memory_space=pltpu.VMEM)
    rows = sum(p.shape[0] for p in parts)
    return pl.pallas_call(
        stack_kernel,
        out_shape=jax.ShapeDtypeStruct((rows, D), jnp.bfloat16),
        in_specs=[vmem] * len(parts),
        out_specs=vmem,
        compiler_params=pltpu.CompilerParams(vmem_limit_bytes=8 * MIB),
        cost_estimate=pl.CostEstimate(flops=0, bytes_accessed=4 * rows * D, transcendentals=0),
        name="stack",
    )(*parts)


def combine_kernel(code_ref, attn_ref, r0, r1, r2, r3, out_ref):
    rows_at = lax.broadcasted_iota(jnp.int32, (ROWS, TOK), 0)
    code = code_ref[...]
    for q in range(4):
        c = slice(q * QUARTER, (q + 1) * QUARTER)
        total = attn_ref[:, c].astype(jnp.float32)
        for i, r in enumerate((r0, r1, r2, r3)):
            pick = (rows_at == code - i * ROWS + q * CAP).astype(jnp.bfloat16)
            total += lax.dot_general(pick, r[...], (((0,), (0,)), ((), ())), preferred_element_type=jnp.float32)
        out_ref[:, c] = total.astype(jnp.bfloat16)


def combine(code, attn, rows):
    vmem = pl.BlockSpec(memory_space=pltpu.VMEM)
    return pl.pallas_call(
        combine_kernel,
        out_shape=jax.ShapeDtypeStruct((TOK, D), jnp.bfloat16),
        in_specs=[vmem] * 6,
        out_specs=vmem,
        compiler_params=pltpu.CompilerParams(vmem_limit_bytes=14 * MIB),
        cost_estimate=pl.CostEstimate(flops=60_000_000, bytes_accessed=3_000_000, transcendentals=0),
        name="combine",
    )(code, attn, *rows)


def same_row(i, q):
    whole = lax.broadcasted_iota(jnp.int32, (ROWS, ROWS), 0) - i * CAP
    quarter = lax.broadcasted_iota(jnp.int32, (ROWS, ROWS), 1) - q * CAP
    return ((whole == quarter) & (whole >= 0) & (whole < CAP)).astype(jnp.bfloat16)


def unpack_kernel(p0, p1, p2, p3, out_ref):
    for q in range(4):
        total = None
        for i, p in enumerate((p0, p1, p2, p3)):
            term = jnp.dot(same_row(i, q), p[...], preferred_element_type=jnp.float32)
            total = term if total is None else total + term
        out_ref[:, q * QUARTER:(q + 1) * QUARTER] = total.astype(jnp.bfloat16)


def unpack(pieces):
    vmem = pl.BlockSpec(memory_space=pltpu.VMEM)
    return pl.pallas_call(
        unpack_kernel,
        out_shape=jax.ShapeDtypeStruct((ROWS, D), jnp.bfloat16),
        in_specs=[vmem] * 4,
        out_specs=vmem,
        compiler_params=pltpu.CompilerParams(vmem_limit_bytes=8 * MIB),
        cost_estimate=pl.CostEstimate(flops=2 * 4 * ROWS * ROWS * D, bytes_accessed=4 * ROWS * D, transcendentals=0),
        name="unpack",
    )(*pieces)


def add_and_pack_kernel(a, b, c, d, *outs):
    totals = [None] * 4
    for q in range(4):
        at = slice(q * QUARTER, (q + 1) * QUARTER)
        rows = sum(r[:, at].astype(jnp.float32) for r in (a, b, c, d)).astype(jnp.bfloat16)
        for i in range(4):
            term = lax.dot_general(same_row(i, q), rows, (((0,), (0,)), ((), ())), preferred_element_type=jnp.float32)
            totals[i] = term if totals[i] is None else totals[i] + term
    for o, total in zip(outs, totals):
        o[...] = total.astype(jnp.bfloat16)


def add_and_pack(parts):
    vmem = pl.BlockSpec(memory_space=pltpu.VMEM)
    return pl.pallas_call(
        add_and_pack_kernel,
        out_shape=tuple(jax.ShapeDtypeStruct((ROWS, QUARTER), jnp.bfloat16) for _ in range(4)),
        in_specs=[vmem] * 4,
        out_specs=(vmem,) * 4,
        compiler_params=pltpu.CompilerParams(vmem_limit_bytes=8 * MIB),
        cost_estimate=pl.CostEstimate(flops=2 * 4 * ROWS * ROWS * D, bytes_accessed=10 * ROWS * D, transcendentals=0),
        name="add_and_pack",
    )(*parts)


def add_up(parts):
    total = parts[0].astype(jnp.float32)
    for p in parts[1:]:
        total = total + p.astype(jnp.float32)
    return total.astype(jnp.bfloat16)


def after(value, *others):
    return lax.optimization_barrier((value, others))[0]


def per_device(queries, key_rows, value_rows, segments, swap_flags, expert_ids, norm_gain, gate_weight, up_weight, down_weight):
    dp = lax.axis_index("dp")
    z = lax.axis_index("expert") // 16
    info = jnp.stack([swap_flags[0], z // 2, 1 - 2 * (z % 2), dp]).astype(jnp.int32)

    across = device_pairs(lambda d, zz, y, x: (d, zz ^ 1, y, x))
    beside = device_pairs(lambda d, zz, y, x: (1 - d, zz, y, x))
    g_first = send(lax.dynamic_slice_in_dim(gate_weight, dp * HALF, CUT, 0), across)

    seg_local = segments.astype(jnp.bfloat16)
    q1, k1, v1, s1 = (send(a, beside) for a in (queries, key_rows, value_rows, seg_local))
    seg = jnp.where(swap_flags[0] > 0, s1, seg_local)[0].astype(jnp.float32)
    position = jnp.arange(TOK)
    allowed = (seg[:, None] == seg[None, :]) & (position[:, None] >= position[None, :])
    bias = jnp.where(allowed, jnp.float32(0), jnp.float32(-1e30))
    attn, code, *rows = attention(
        info, queries, q1, key_rows, k1, value_rows, v1, bias, expert_ids.reshape(1, TOK), norm_gain.reshape(1, D)
    )

    moved = [send(rows[k], to_expert(k)) for k in (1, 2, 3)]
    mine = unpack([rows[0]] + after(moved, g_first))
    g_rest = lax.dynamic_slice_in_dim(gate_weight, dp * HALF + CUT, HALF - CUT, 0)
    g_rest = send(after(g_rest, code), across)
    line = stack([mine] + [send(mine, plane_shift(1, s)) for s in (1, 3, 2)])
    c1, c3, c2 = (send(line, plane_shift(2, s)) for s in (1, 3, 2))
    u_half = lax.dynamic_slice_in_dim(up_weight, dp * HALF, HALF, 0)
    u_half = send(after(u_half, moved), across)

    own_gu = (gate_weight, up_weight)
    g_rest = hold(g_rest, 3 * HINT // 2)
    h_line = hidden(info, [after(line, g_rest)], ("own",), own_gu)
    g_first, g_rest, u_half = after((g_first, g_rest, u_half), h_line)
    other_gu = (g_first, g_rest, send(g_first, beside), send(g_rest, beside), u_half, send(u_half, beside))
    h_near = hidden(info, [c1, c3], ("own",), own_gu, HINT)
    wa = send(after(lax.dynamic_slice_in_dim(down_weight, dp * (FF // 2), FF // 2, 0), line), across)
    h_other = hidden(info, [after(line, h_near), c1, c3], ("other",), other_gu)
    wa = hold(after(wa, (h_other, c2)), 3*HINT//2)
    h_last = hidden(info, [after(c2, wa)], ("own", "other"), own_gu + other_gu)
    hs = (h_line, h_near, h_other, h_last)

    outs0, outs1 = down(info, hs, down_weight, wa, send(wa, beside))

    relay0 = send(outs0[3], plane_shift(2, 1))
    relay1 = send(outs1[3], plane_shift(2, 3))
    plain0 = send(outs0[1], plane_shift(2, 3))
    plain1 = send(outs1[2], plane_shift(2, 1))
    both0 = send(add_up([outs0[2], relay0]), plane_shift(2, 1))
    both1 = send(add_up([outs1[1], relay1]), plane_shift(2, 3))
    halves = ((outs0[0], plain0, both0), (outs1[0], plain1, both1))
    back = line_sums(halves)
    pieces = add_and_pack([back[0]] + [send(b, plane_shift(1, s)) for b, s in zip(back[1:], (3, 1, 2))])
    returned = [pieces[0]] + [send(pieces[k], reverse(to_expert(k))) for k in (1, 2, 3)]
    return combine(code, attn, returned)


def solution(mesh):
    in_specs = (
        P(("dp", "expert"), None),
        P(("dp", "expert"), None),
        P(("dp", "expert"), None),
        P(("dp", "expert"), None),
        P("expert"),
        P(("dp", "expert"), None),
        P(),
        P(None, "expert"),
        P(None, "expert"),
        P("expert", None),
    )
    out_specs = P(("dp", "expert"), None)
    return jax.shard_map(
        per_device, mesh=mesh, in_specs=in_specs, out_specs=out_specs, check_vma=False
    )
```

```python
import functools
import itertools

import jax
import jax.numpy as jnp
from jax import lax
from jax.experimental import pallas as pl
from jax.experimental.pallas import tpu as pltpu
from jax.sharding import PartitionSpec as P

HEADS = 40
KVH = 8
GROUP = HEADS // KVH
HD = 128
D = 5120
FF = 256
EXP_WIN = 4
CAP = 10
TOK = 128
ROWS = EXP_WIN * CAP
LINE = 4 * ROWS
HALF = D // 2
QUARTER = D // 4
CUT = 1280
ALL = ("dp", "expert")
MIB = 1 << 20
HINT = 6_000_000_000


def device_pairs(target):
    pairs = []
    for dp, z, y, x in itertools.product(range(2), range(8), range(4), range(4)):
        to = target(dp, z, y, x)
        pairs.append((((dp * 8 + z) * 4 + y) * 4 + x, ((to[0] * 8 + to[1]) * 4 + to[2]) * 4 + to[3]))
    return pairs


def plane_shift(phase, step):
    def target(dp, z, y, x):
        if (dp == 0) == (phase == 1):
            return dp, z, y, (x + step) % 4
        return dp, z, (y + step) % 4, x

    return device_pairs(target)


def to_expert(kind):
    offset = {1: (2, -2), 2: (-3, 3), 3: (-1, 1)}[kind]
    return device_pairs(lambda dp, z, y, x: (dp, (z + offset[z % 2]) % 8, y, x))


def reverse(pairs):
    return [(b, a) for a, b in pairs]


def send(value, pairs):
    return lax.ppermute(value, ALL, pairs)


def attention_kernel(info, q0, q1, k0, k1, v0, v1, bias_ref, route_ref, gain_ref, attn_ref, code_ref, b0, b1, b2, b3, acc, q, k, v, sem):
    kept = [pltpu.make_async_copy(a, b, sem.at[i]) for i, (a, b) in enumerate(((k0, k), (q0, q), (v0, v)))]
    swapped = [pltpu.make_async_copy(a, b, sem.at[i]) for i, (a, b) in enumerate(((k1, k), (q1, q), (v1, v)))]

    @pl.when(info[0] > 0)
    def _():
        for c in swapped:
            c.start()

    @pl.when(info[0] <= 0)
    def _():
        for c in kept:
            c.start()

    bias = bias_ref[...]
    acc[...] = jnp.zeros_like(acc)
    for c in kept:
        c.wait()
    for h in range(KVH):
        cols = slice(h * HD, (h + 1) * HD)
        key = k[:, cols]
        value = v[:, cols]
        heads = [slice((h * GROUP + g) * HD, (h * GROUP + g + 1) * HD) for g in range(GROUP)]
        query = jnp.concatenate([q[:, c] for c in heads], axis=0)
        scores = lax.dot_general(query, key, (((1,), (1,)), ((), ())), preferred_element_type=jnp.float32)
        scores = scores.reshape(GROUP, TOK, TOK) * HD ** (-0.5) + bias[None]
        top = jnp.max(scores, axis=-1, keepdims=True)
        expo = jnp.exp(scores - top)
        probs = (expo * (1.0 / jnp.sum(expo, axis=-1, keepdims=True))).astype(jnp.bfloat16)
        mixed = jnp.dot(probs.reshape(GROUP * TOK, TOK), value, preferred_element_type=jnp.float32)
        mixed = mixed.astype(jnp.bfloat16)
        for g, c in enumerate(heads):
            part = mixed[g * TOK:(g + 1) * TOK]
            attn_ref[:, c] = part
            part_f = part.astype(jnp.float32)
            acc[...] += part_f * part_f
    scale = lax.rsqrt(jnp.sum(acc[...], axis=-1, keepdims=True) * (1.0 / D) + 1e-05)
    route = route_ref[...]
    kind = jnp.where(route < EXP_WIN, ((route - info[1]) * info[2]) & 3, 64)
    lanes = lax.broadcasted_iota(jnp.int32, (TOK, TOK), 1)
    earlier = (lax.broadcasted_iota(jnp.int32, (TOK, TOK), 0) < lanes).astype(jnp.bfloat16)
    chosen = (lax.broadcasted_iota(jnp.int32, (16, TOK), 0) == kind).astype(jnp.bfloat16)
    order = jnp.dot(chosen, earlier, preferred_element_type=jnp.float32)
    slot = jnp.sum(chosen.astype(jnp.float32) * order, axis=0, keepdims=True).astype(jnp.int32)
    code = jnp.where(kind < EXP_WIN, kind * ROWS + slot, -1000)
    code_ref[...] = code
    rows_at = lax.broadcasted_iota(jnp.int32, (4 * ROWS, TOK), 0)
    picks = [(rows_at == code + q * CAP).astype(jnp.bfloat16) for q in range(4)]
    half = QUARTER // 2
    for n in range(2):
        rows = None
        for q in range(4):
            c = slice(q * QUARTER + n * half, q * QUARTER + (n + 1) * half)
            normed = (attn_ref[:, c].astype(jnp.float32) * scale * gain_ref[:, c].astype(jnp.float32)).astype(jnp.bfloat16)
            term = jnp.dot(picks[q], normed, preferred_element_type=jnp.float32)
            rows = term if rows is None else rows + term
        for i, b in enumerate((b0, b1, b2, b3)):
            b[:, n * half:(n + 1) * half] = rows[i * ROWS:(i + 1) * ROWS].astype(jnp.bfloat16)


def attention(info, q0, q1, k0, k1, v0, v1, bias, route, gain):
    vmem = pl.BlockSpec(memory_space=pltpu.VMEM)
    rows = jax.ShapeDtypeStruct((ROWS, QUARTER), jnp.bfloat16)
    return pl.pallas_call(
        attention_kernel,
        out_shape=(
            jax.ShapeDtypeStruct((TOK, D), jnp.bfloat16),
            jax.ShapeDtypeStruct((1, TOK), jnp.int32),
            rows, rows, rows, rows,
        ),
        in_specs=[pl.BlockSpec(memory_space=pltpu.SMEM)] + [pl.BlockSpec(memory_space=pl.ANY)] * 6 + [vmem] * 3,
        out_specs=(vmem,) * 6,
        scratch_shapes=[
            pltpu.VMEM((TOK, TOK), jnp.float32),
            pltpu.VMEM((TOK, D), jnp.bfloat16),
            pltpu.VMEM((TOK, KVH * HD), jnp.bfloat16),
            pltpu.VMEM((TOK, KVH * HD), jnp.bfloat16),
            pltpu.SemaphoreType.DMA((3,)),
        ],
        compiler_params=pltpu.CompilerParams(vmem_limit_bytes=56 * MIB),
        cost_estimate=pl.CostEstimate(flops=400_000_000, bytes_accessed=6_000_000, transcendentals=660_000),
        name="attention",
    )(info, q0, q1, k0, k1, v0, v1, bias, route, gain)


def silu_mul(gate, up):
    return (gate / (1.0 + jnp.exp(-gate)) * up).astype(jnp.bfloat16)


def hidden_kernel(count, parts, info, *refs):
    xs, srcs, h_refs = refs[:count], list(refs[count:-len(parts)]), refs[-len(parts):]
    near = info[3] * HALF
    far = HALF - near
    for i, part in enumerate(parts):
        if part == "own":
            g, u = (srcs.pop(0) for _ in range(2))
            pieces = [(g.at[pl.ds(k, CUT)], u.at[pl.ds(k, CUT)], k) for k in range(0, D, CUT)]
        else:
            ga1, ga2, gb1, gb2, ua, ub = (srcs.pop(0) for _ in range(6))
            head, tail = pl.ds(0, CUT), pl.ds(CUT, CUT)
            pieces = [
                (ga1, ua.at[head], near),
                (ga2, ua.at[tail], near + CUT),
                (gb1, ub.at[head], far),
                (gb2, ub.at[tail], far + CUT),
            ]
        gate = up = None
        for g, u, k in pieces:
            at = pl.ds(k if isinstance(k, int) else pl.multiple_of(k, HD), CUT)
            x = jnp.concatenate([r[:, at] for r in xs], axis=0)
            gate_term = jnp.dot(x, g[...], preferred_element_type=jnp.float32)
            up_term = jnp.dot(x, u[...], preferred_element_type=jnp.float32)
            gate, up = (gate_term, up_term) if gate is None else (gate + gate_term, up + up_term)
        h_refs[i][...] = silu_mul(gate, up)


def hidden(info, xs, parts, weights, flops=0):
    count, n = len(xs), len(parts)
    vmem = pl.BlockSpec(memory_space=pltpu.VMEM)
    total = count * LINE
    return pl.pallas_call(
        functools.partial(hidden_kernel, count, parts),
        out_shape=tuple(jax.ShapeDtypeStruct((total, FF), jnp.bfloat16) for _ in parts),
        in_specs=[pl.BlockSpec(memory_space=pltpu.SMEM)] + [vmem] * (count + len(weights)),
        out_specs=(vmem,) * n,
        compiler_params=pltpu.CompilerParams(vmem_limit_bytes=18 * MIB),
        cost_estimate=pl.CostEstimate(flops=max(flops, 4 * total * D * n * FF), bytes_accessed=4 * D * n * FF + 2 * total * D, transcendentals=total * n * FF),
        name="hidden",
    )(info, *xs, *weights)


def down_kernel(n_own, info, *refs):
    chunks = (len(refs) - 4 - n_own) // 2
    own_refs, other_ref, (own_w, wa, wb), outs = refs[:n_own], refs[n_own], refs[n_own + 1:n_own + 4], refs[n_own + 4:]
    near = pl.ds(pl.multiple_of(info[3] * (FF // 2), FF // 2), FF // 2)
    far = pl.ds(pl.multiple_of((1 - info[3]) * (FF // 2), FF // 2), FF // 2)
    own = jnp.concatenate([r[...] for r in own_refs], axis=0)
    h = jnp.concatenate([own, other_ref[:, near], other_ref[:, far]], axis=1)
    tile = 512
    for n in range(D // tile):
        cols = pl.ds(n * tile, tile)
        w = jnp.concatenate([own_w[:, cols], wa[:, cols], wb[:, cols]], axis=0)
        y = jnp.dot(h, w, preferred_element_type=jnp.float32).astype(jnp.bfloat16)
        half, at = divmod(n * tile, HALF)
        for i in range(chunks):
            outs[chunks * half + i][:, at:at + tile] = y[i * LINE:(i + 1) * LINE]


def down(info, own, other, own_w, wa, wb):
    vmem = pl.BlockSpec(memory_space=pltpu.VMEM)
    total = other.shape[0]
    chunks = total // LINE
    outs = pl.pallas_call(
        functools.partial(down_kernel, len(own)),
        out_shape=tuple(jax.ShapeDtypeStruct((LINE, HALF), jnp.bfloat16) for _ in range(2 * chunks)),
        in_specs=[pl.BlockSpec(memory_space=pltpu.SMEM)] + [vmem] * (len(own) + 4),
        out_specs=(vmem,) * (2 * chunks),
        compiler_params=pltpu.CompilerParams(vmem_limit_bytes=20 * MIB),
        cost_estimate=pl.CostEstimate(flops=2 * total * 2 * FF * D, bytes_accessed=4 * FF * D + 2 * total * D, transcendentals=0),
        name="down",
    )(info, *own, other, own_w, wa, wb)
    return outs[:chunks], outs[chunks:]


def hold(value, flops):
    hbm = pl.BlockSpec(memory_space=pl.ANY)
    return pl.pallas_call(
        lambda value_ref, out_ref: None,
        out_shape=jax.ShapeDtypeStruct(value.shape, value.dtype),
        in_specs=[hbm],
        out_specs=hbm,
        input_output_aliases={0: 0},
        compiler_params=pltpu.CompilerParams(vmem_limit_bytes=MIB),
        cost_estimate=pl.CostEstimate(flops=flops, bytes_accessed=0, transcendentals=0),
        name="hold",
    )(value)


def line_sums_kernel(*refs):
    parts, outs = refs[:6], refs[6:]
    tile = 512
    for n in range(D // tile):
        half, at = divmod(n * tile, HALF)
        a, b, c = (r[:, at:at + tile].astype(jnp.float32) for r in parts[3 * half:3 * half + 3])
        total = a + b + c
        for i, o in enumerate(outs):
            o[:, n * tile:(n + 1) * tile] = total[i * ROWS:(i + 1) * ROWS].astype(jnp.bfloat16)


def line_sums(halves):
    vmem = pl.BlockSpec(memory_space=pltpu.VMEM)
    return pl.pallas_call(
        line_sums_kernel,
        out_shape=tuple(jax.ShapeDtypeStruct((ROWS, D), jnp.bfloat16) for _ in range(4)),
        in_specs=[vmem] * 6,
        out_specs=(vmem,) * 4,
        compiler_params=pltpu.CompilerParams(vmem_limit_bytes=12 * MIB),
        cost_estimate=pl.CostEstimate(flops=2 * LINE * D, bytes_accessed=8 * LINE * D, transcendentals=0),
        name="line_sums",
    )(*halves[0], *halves[1])


def stack_kernel(*refs):
    at = 0
    for r in refs[:-1]:
        refs[-1][at:at + r.shape[0], :] = r[...]
        at += r.shape[0]


def stack(parts):
    vmem = pl.BlockSpec(memory_space=pltpu.VMEM)
    rows = sum(p.shape[0] for p in parts)
    return pl.pallas_call(
        stack_kernel,
        out_shape=jax.ShapeDtypeStruct((rows, D), jnp.bfloat16),
        in_specs=[vmem] * len(parts),
        out_specs=vmem,
        compiler_params=pltpu.CompilerParams(vmem_limit_bytes=8 * MIB),
        cost_estimate=pl.CostEstimate(flops=0, bytes_accessed=4 * rows * D, transcendentals=0),
        name="stack",
    )(*parts)


def combine_kernel(code_ref, attn_ref, r0, r1, r2, r3, out_ref):
    rows_at = lax.broadcasted_iota(jnp.int32, (ROWS, TOK), 0)
    code = code_ref[...]
    for q in range(4):
        c = slice(q * QUARTER, (q + 1) * QUARTER)
        total = attn_ref[:, c].astype(jnp.float32)
        for i, r in enumerate((r0, r1, r2, r3)):
            pick = (rows_at == code - i * ROWS + q * CAP).astype(jnp.bfloat16)
            total += lax.dot_general(pick, r[...], (((0,), (0,)), ((), ())), preferred_element_type=jnp.float32)
        out_ref[:, c] = total.astype(jnp.bfloat16)


def combine(code, attn, rows):
    vmem = pl.BlockSpec(memory_space=pltpu.VMEM)
    return pl.pallas_call(
        combine_kernel,
        out_shape=jax.ShapeDtypeStruct((TOK, D), jnp.bfloat16),
        in_specs=[vmem] * 6,
        out_specs=vmem,
        compiler_params=pltpu.CompilerParams(vmem_limit_bytes=14 * MIB),
        cost_estimate=pl.CostEstimate(flops=60_000_000, bytes_accessed=3_000_000, transcendentals=0),
        name="combine",
    )(code, attn, *rows)


def same_row(i, q):
    whole = lax.broadcasted_iota(jnp.int32, (ROWS, ROWS), 0) - i * CAP
    quarter = lax.broadcasted_iota(jnp.int32, (ROWS, ROWS), 1) - q * CAP
    return ((whole == quarter) & (whole >= 0) & (whole < CAP)).astype(jnp.bfloat16)


def unpack_kernel(p0, p1, p2, p3, out_ref):
    for q in range(4):
        total = None
        for i, p in enumerate((p0, p1, p2, p3)):
            term = jnp.dot(same_row(i, q), p[...], preferred_element_type=jnp.float32)
            total = term if total is None else total + term
        out_ref[:, q * QUARTER:(q + 1) * QUARTER] = total.astype(jnp.bfloat16)


def unpack(pieces):
    vmem = pl.BlockSpec(memory_space=pltpu.VMEM)
    return pl.pallas_call(
        unpack_kernel,
        out_shape=jax.ShapeDtypeStruct((ROWS, D), jnp.bfloat16),
        in_specs=[vmem] * 4,
        out_specs=vmem,
        compiler_params=pltpu.CompilerParams(vmem_limit_bytes=8 * MIB),
        cost_estimate=pl.CostEstimate(flops=2 * 4 * ROWS * ROWS * D, bytes_accessed=4 * ROWS * D, transcendentals=0),
        name="unpack",
    )(*pieces)


def add_and_pack_kernel(a, b, c, d, *outs):
    totals = [None] * 4
    for q in range(4):
        at = slice(q * QUARTER, (q + 1) * QUARTER)
        rows = sum(r[:, at].astype(jnp.float32) for r in (a, b, c, d)).astype(jnp.bfloat16)
        for i in range(4):
            term = lax.dot_general(same_row(i, q), rows, (((0,), (0,)), ((), ())), preferred_element_type=jnp.float32)
            totals[i] = term if totals[i] is None else totals[i] + term
    for o, total in zip(outs, totals):
        o[...] = total.astype(jnp.bfloat16)


def add_and_pack(parts):
    vmem = pl.BlockSpec(memory_space=pltpu.VMEM)
    return pl.pallas_call(
        add_and_pack_kernel,
        out_shape=tuple(jax.ShapeDtypeStruct((ROWS, QUARTER), jnp.bfloat16) for _ in range(4)),
        in_specs=[vmem] * 4,
        out_specs=(vmem,) * 4,
        compiler_params=pltpu.CompilerParams(vmem_limit_bytes=8 * MIB),
        cost_estimate=pl.CostEstimate(flops=2 * 4 * ROWS * ROWS * D, bytes_accessed=10 * ROWS * D, transcendentals=0),
        name="add_and_pack",
    )(*parts)


def add_up(parts):
    total = parts[0].astype(jnp.float32)
    for p in parts[1:]:
        total = total + p.astype(jnp.float32)
    return total.astype(jnp.bfloat16)


def after(value, *others):
    return lax.optimization_barrier((value, others))[0]


def per_device(queries, key_rows, value_rows, segments, swap_flags, expert_ids, norm_gain, gate_weight, up_weight, down_weight):
    dp = lax.axis_index("dp")
    z = lax.axis_index("expert") // 16
    info = jnp.stack([swap_flags[0], z // 2, 1 - 2 * (z % 2), dp]).astype(jnp.int32)

    across = device_pairs(lambda d, zz, y, x: (d, zz ^ 1, y, x))
    beside = device_pairs(lambda d, zz, y, x: (1 - d, zz, y, x))
    g_first = send(lax.dynamic_slice_in_dim(gate_weight, dp * HALF, CUT, 0), across)

    seg_local = segments.astype(jnp.bfloat16)
    q1, k1, v1, s1 = (send(a, beside) for a in (queries, key_rows, value_rows, seg_local))
    seg = jnp.where(swap_flags[0] > 0, s1, seg_local)[0].astype(jnp.float32)
    position = jnp.arange(TOK)
    allowed = (seg[:, None] == seg[None, :]) & (position[:, None] >= position[None, :])
    bias = jnp.where(allowed, jnp.float32(0), jnp.float32(-1e30))
    attn, code, *rows = attention(
        info, queries, q1, key_rows, k1, value_rows, v1, bias, expert_ids.reshape(1, TOK), norm_gain.reshape(1, D)
    )

    moved = [send(rows[k], to_expert(k)) for k in (1, 2, 3)]
    mine = unpack([rows[0]] + after(moved, g_first))
    g_rest = lax.dynamic_slice_in_dim(gate_weight, dp * HALF + CUT, HALF - CUT, 0)
    g_rest = send(after(g_rest, code), across)
    line = stack([mine] + [send(mine, plane_shift(1, s)) for s in (1, 3, 2)])
    c1, c3, c2 = (send(line, plane_shift(2, s)) for s in (1, 3, 2))
    u_half = lax.dynamic_slice_in_dim(up_weight, dp * HALF, HALF, 0)
    u_half = send(after(u_half, moved), across)

    own_gu = (gate_weight, up_weight)
    g_rest = hold(g_rest, 3 * HINT // 2)
    (h_line,) = hidden(info, [after(line, g_rest)], ("own",), own_gu)
    g_first, g_rest, u_half = after((g_first, g_rest, u_half), h_line)
    other_gu = (g_first, g_rest, send(g_first, beside), send(g_rest, beside), u_half, send(u_half, beside))
    (h_near,) = hidden(info, [c1, c3], ("own",), own_gu, HINT)
    wa = send(after(lax.dynamic_slice_in_dim(down_weight, dp * (FF // 2), FF // 2, 0), line), across)
    (h_other,) = hidden(info, [after(line, h_near), c1, c3], ("other",), other_gu)
    wa = hold(after(wa, (h_other, c2)), 3*HINT//2)
    own_last, other_last = hidden(info, [after(c2, wa)], ("own", "other"), own_gu + other_gu)

    wb = send(wa, beside)
    (far0,), (far1,) = down(info, [own_last], other_last, down_weight, wa, wb)
    outs0, outs1 = down(info, [h_line, h_near], h_other, down_weight, wa, after(wb, far0))

    relay0 = send(far0, plane_shift(2, 1))
    relay1 = send(far1, plane_shift(2, 3))
    plain0 = send(outs0[1], plane_shift(2, 3))
    plain1 = send(outs1[2], plane_shift(2, 1))
    both0 = send(add_up([outs0[2], relay0]), plane_shift(2, 1))
    both1 = send(add_up([outs1[1], relay1]), plane_shift(2, 3))
    halves = ((outs0[0], plain0, both0), (outs1[0], plain1, both1))
    back = line_sums(halves)
    pieces = add_and_pack([back[0]] + [send(b, plane_shift(1, s)) for b, s in zip(back[1:], (3, 1, 2))])
    returned = [pieces[0]] + [send(pieces[k], reverse(to_expert(k))) for k in (1, 2, 3)]
    return combine(code, attn, returned)


def solution(mesh):
    in_specs = (
        P(("dp", "expert"), None),
        P(("dp", "expert"), None),
        P(("dp", "expert"), None),
        P(("dp", "expert"), None),
        P("expert"),
        P(("dp", "expert"), None),
        P(),
        P(None, "expert"),
        P(None, "expert"),
        P("expert", None),
    )
    out_specs = P(("dp", "expert"), None)
    return jax.shard_map(
        per_device, mesh=mesh, in_specs=in_specs, out_specs=out_specs, check_vma=False
    )
```

```python
import functools
import itertools

import jax
import jax.numpy as jnp
from jax import lax
from jax.experimental import pallas as pl
from jax.experimental.pallas import tpu as pltpu
from jax.sharding import PartitionSpec as P

HEADS = 40
KVH = 8
GROUP = HEADS // KVH
HD = 128
D = 5120
FF = 256
EXP_WIN = 4
CAP = 10
TOK = 128
ROWS = EXP_WIN * CAP
LINE = 4 * ROWS
HALF = D // 2
QUARTER = D // 4
CUT = 1280
ALL = ("dp", "expert")
MIB = 1 << 20
HINT = 6_000_000_000


def device_pairs(target):
    pairs = []
    for dp, z, y, x in itertools.product(range(2), range(8), range(4), range(4)):
        to = target(dp, z, y, x)
        pairs.append((((dp * 8 + z) * 4 + y) * 4 + x, ((to[0] * 8 + to[1]) * 4 + to[2]) * 4 + to[3]))
    return pairs


def plane_shift(phase, step):
    def target(dp, z, y, x):
        if (dp == 0) == (phase == 1):
            return dp, z, y, (x + step) % 4
        return dp, z, (y + step) % 4, x

    return device_pairs(target)


def to_expert(kind):
    offset = {1: (2, -2), 2: (-3, 3), 3: (-1, 1)}[kind]
    return device_pairs(lambda dp, z, y, x: (dp, (z + offset[z % 2]) % 8, y, x))


def reverse(pairs):
    return [(b, a) for a, b in pairs]


def send(value, pairs):
    return lax.ppermute(value, ALL, pairs)


def attention_kernel(info, q0, q1, k0, k1, v0, v1, bias_ref, route_ref, gain_ref, attn_ref, code_ref, b0, b1, b2, b3, acc, q, k, v, sem):
    kept = [pltpu.make_async_copy(a, b, sem.at[i]) for i, (a, b) in enumerate(((k0, k), (q0, q), (v0, v)))]
    swapped = [pltpu.make_async_copy(a, b, sem.at[i]) for i, (a, b) in enumerate(((k1, k), (q1, q), (v1, v)))]

    @pl.when(info[0] > 0)
    def _():
        for c in swapped:
            c.start()

    @pl.when(info[0] <= 0)
    def _():
        for c in kept:
            c.start()

    bias = bias_ref[...]
    acc[...] = jnp.zeros_like(acc)
    for c in kept:
        c.wait()
    for h in range(KVH):
        cols = slice(h * HD, (h + 1) * HD)
        key = k[:, cols]
        value = v[:, cols]
        heads = [slice((h * GROUP + g) * HD, (h * GROUP + g + 1) * HD) for g in range(GROUP)]
        query = jnp.concatenate([q[:, c] for c in heads], axis=0)
        scores = lax.dot_general(query, key, (((1,), (1,)), ((), ())), preferred_element_type=jnp.float32)
        scores = scores.reshape(GROUP, TOK, TOK) * HD ** (-0.5) + bias[None]
        top = jnp.max(scores, axis=-1, keepdims=True)
        expo = jnp.exp(scores - top)
        probs = (expo * (1.0 / jnp.sum(expo, axis=-1, keepdims=True))).astype(jnp.bfloat16)
        mixed = jnp.dot(probs.reshape(GROUP * TOK, TOK), value, preferred_element_type=jnp.float32)
        mixed = mixed.astype(jnp.bfloat16)
        for g, c in enumerate(heads):
            part = mixed[g * TOK:(g + 1) * TOK]
            attn_ref[:, c] = part
            part_f = part.astype(jnp.float32)
            acc[...] += part_f * part_f
    scale = lax.rsqrt(jnp.sum(acc[...], axis=-1, keepdims=True) * (1.0 / D) + 1e-05)
    route = route_ref[...]
    kind = jnp.where(route < EXP_WIN, ((route - info[1]) * info[2]) & 3, 64)
    lanes = lax.broadcasted_iota(jnp.int32, (TOK, TOK), 1)
    earlier = (lax.broadcasted_iota(jnp.int32, (TOK, TOK), 0) < lanes).astype(jnp.bfloat16)
    chosen = (lax.broadcasted_iota(jnp.int32, (16, TOK), 0) == kind).astype(jnp.bfloat16)
    order = jnp.dot(chosen, earlier, preferred_element_type=jnp.float32)
    slot = jnp.sum(chosen.astype(jnp.float32) * order, axis=0, keepdims=True).astype(jnp.int32)
    code = jnp.where(kind < EXP_WIN, kind * ROWS + slot, -1000)
    code_ref[...] = code
    rows_at = lax.broadcasted_iota(jnp.int32, (4 * ROWS, TOK), 0)
    picks = [(rows_at == code + q * CAP).astype(jnp.bfloat16) for q in range(4)]
    half = QUARTER // 2
    for n in range(2):
        rows = None
        for q in range(4):
            c = slice(q * QUARTER + n * half, q * QUARTER + (n + 1) * half)
            normed = (attn_ref[:, c].astype(jnp.float32) * scale * gain_ref[:, c].astype(jnp.float32)).astype(jnp.bfloat16)
            term = jnp.dot(picks[q], normed, preferred_element_type=jnp.float32)
            rows = term if rows is None else rows + term
        for i, b in enumerate((b0, b1, b2, b3)):
            b[:, n * half:(n + 1) * half] = rows[i * ROWS:(i + 1) * ROWS].astype(jnp.bfloat16)


def attention(info, q0, q1, k0, k1, v0, v1, bias, route, gain):
    vmem = pl.BlockSpec(memory_space=pltpu.VMEM)
    rows = jax.ShapeDtypeStruct((ROWS, QUARTER), jnp.bfloat16)
    return pl.pallas_call(
        attention_kernel,
        out_shape=(
            jax.ShapeDtypeStruct((TOK, D), jnp.bfloat16),
            jax.ShapeDtypeStruct((1, TOK), jnp.int32),
            rows, rows, rows, rows,
        ),
        in_specs=[pl.BlockSpec(memory_space=pltpu.SMEM)] + [pl.BlockSpec(memory_space=pl.ANY)] * 6 + [vmem] * 3,
        out_specs=(vmem,) * 6,
        scratch_shapes=[
            pltpu.VMEM((TOK, TOK), jnp.float32),
            pltpu.VMEM((TOK, D), jnp.bfloat16),
            pltpu.VMEM((TOK, KVH * HD), jnp.bfloat16),
            pltpu.VMEM((TOK, KVH * HD), jnp.bfloat16),
            pltpu.SemaphoreType.DMA((3,)),
        ],
        compiler_params=pltpu.CompilerParams(vmem_limit_bytes=56 * MIB),
        cost_estimate=pl.CostEstimate(flops=400_000_000, bytes_accessed=6_000_000, transcendentals=660_000),
        name="attention",
    )(info, q0, q1, k0, k1, v0, v1, bias, route, gain)


def silu_mul(gate, up):
    return (gate / (1.0 + jnp.exp(-gate)) * up).astype(jnp.bfloat16)


def hidden_kernel(count, parts, info, *refs):
    xs, srcs, h_refs = refs[:count], list(refs[count:-len(parts)]), refs[-len(parts):]
    near = info[3] * HALF
    far = HALF - near
    for i, part in enumerate(parts):
        if part == "own":
            g, u = (srcs.pop(0) for _ in range(2))
            pieces = [(g.at[pl.ds(k, CUT)], u.at[pl.ds(k, CUT)], k) for k in range(0, D, CUT)]
        else:
            ga1, ga2, gb1, gb2, ua, ub = (srcs.pop(0) for _ in range(6))
            head, tail = pl.ds(0, CUT), pl.ds(CUT, CUT)
            pieces = [
                (ga1, ua.at[head], near),
                (ga2, ua.at[tail], near + CUT),
                (gb1, ub.at[head], far),
                (gb2, ub.at[tail], far + CUT),
            ]
        gate = up = None
        for g, u, k in pieces:
            at = pl.ds(k if isinstance(k, int) else pl.multiple_of(k, HD), CUT)
            x = jnp.concatenate([r[:, at] for r in xs], axis=0)
            gate_term = jnp.dot(x, g[...], preferred_element_type=jnp.float32)
            up_term = jnp.dot(x, u[...], preferred_element_type=jnp.float32)
            gate, up = (gate_term, up_term) if gate is None else (gate + gate_term, up + up_term)
        h_refs[i][...] = silu_mul(gate, up)


def hidden(info, xs, parts, weights, flops=0):
    count, n = len(xs), len(parts)
    vmem = pl.BlockSpec(memory_space=pltpu.VMEM)
    total = count * LINE
    return pl.pallas_call(
        functools.partial(hidden_kernel, count, parts),
        out_shape=tuple(jax.ShapeDtypeStruct((total, FF), jnp.bfloat16) for _ in parts),
        in_specs=[pl.BlockSpec(memory_space=pltpu.SMEM)] + [vmem] * (count + len(weights)),
        out_specs=(vmem,) * n,
        compiler_params=pltpu.CompilerParams(vmem_limit_bytes=18 * MIB),
        cost_estimate=pl.CostEstimate(flops=max(flops, 4 * total * D * n * FF), bytes_accessed=4 * D * n * FF + 2 * total * D, transcendentals=total * n * FF),
        name="hidden",
    )(info, *xs, *weights)


def down_kernel(n_own, info, *refs):
    chunks = (len(refs) - 4 - n_own) // 2
    own_refs, other_ref, (own_w, wa, wb), outs = refs[:n_own], refs[n_own], refs[n_own + 1:n_own + 4], refs[n_own + 4:]
    near = pl.ds(pl.multiple_of(info[3] * (FF // 2), FF // 2), FF // 2)
    far = pl.ds(pl.multiple_of((1 - info[3]) * (FF // 2), FF // 2), FF // 2)
    own = jnp.concatenate([r[...] for r in own_refs], axis=0)
    h = jnp.concatenate([own, other_ref[:, near], other_ref[:, far]], axis=1)
    tile = 512
    for n in range(D // tile):
        cols = pl.ds(n * tile, tile)
        w = jnp.concatenate([own_w[:, cols], wa[:, cols], wb[:, cols]], axis=0)
        y = jnp.dot(h, w, preferred_element_type=jnp.float32).astype(jnp.bfloat16)
        half, at = divmod(n * tile, HALF)
        for i in range(chunks):
            outs[chunks * half + i][:, at:at + tile] = y[i * LINE:(i + 1) * LINE]


def down(info, own, other, own_w, wa, wb):
    vmem = pl.BlockSpec(memory_space=pltpu.VMEM)
    total = other.shape[0]
    chunks = total // LINE
    outs = pl.pallas_call(
        functools.partial(down_kernel, len(own)),
        out_shape=tuple(jax.ShapeDtypeStruct((LINE, HALF), jnp.bfloat16) for _ in range(2 * chunks)),
        in_specs=[pl.BlockSpec(memory_space=pltpu.SMEM)] + [vmem] * (len(own) + 4),
        out_specs=(vmem,) * (2 * chunks),
        compiler_params=pltpu.CompilerParams(vmem_limit_bytes=20 * MIB),
        cost_estimate=pl.CostEstimate(flops=2 * total * 2 * FF * D, bytes_accessed=4 * FF * D + 2 * total * D, transcendentals=0),
        name="down",
    )(info, *own, other, own_w, wa, wb)
    return outs[:chunks], outs[chunks:]


def hold(value, flops):
    hbm = pl.BlockSpec(memory_space=pl.ANY)
    return pl.pallas_call(
        lambda value_ref, out_ref: None,
        out_shape=jax.ShapeDtypeStruct(value.shape, value.dtype),
        in_specs=[hbm],
        out_specs=hbm,
        input_output_aliases={0: 0},
        compiler_params=pltpu.CompilerParams(vmem_limit_bytes=MIB),
        cost_estimate=pl.CostEstimate(flops=flops, bytes_accessed=0, transcendentals=0),
        name="hold",
    )(value)


def line_sums_kernel(*refs):
    parts, outs = refs[:6], refs[6:]
    tile = 512
    for n in range(D // tile):
        half, at = divmod(n * tile, HALF)
        a, b, c = (r[:, at:at + tile].astype(jnp.float32) for r in parts[3 * half:3 * half + 3])
        total = a + b + c
        for i, o in enumerate(outs):
            o[:, n * tile:(n + 1) * tile] = total[i * ROWS:(i + 1) * ROWS].astype(jnp.bfloat16)


def line_sums(halves):
    vmem = pl.BlockSpec(memory_space=pltpu.VMEM)
    return pl.pallas_call(
        line_sums_kernel,
        out_shape=tuple(jax.ShapeDtypeStruct((ROWS, D), jnp.bfloat16) for _ in range(4)),
        in_specs=[vmem] * 6,
        out_specs=(vmem,) * 4,
        compiler_params=pltpu.CompilerParams(vmem_limit_bytes=12 * MIB),
        cost_estimate=pl.CostEstimate(flops=2 * LINE * D, bytes_accessed=8 * LINE * D, transcendentals=0),
        name="line_sums",
    )(*halves[0], *halves[1])


def stack_kernel(*refs):
    at = 0
    for r in refs[:-1]:
        refs[-1][at:at + r.shape[0], :] = r[...]
        at += r.shape[0]


def stack(parts):
    vmem = pl.BlockSpec(memory_space=pltpu.VMEM)
    rows = sum(p.shape[0] for p in parts)
    return pl.pallas_call(
        stack_kernel,
        out_shape=jax.ShapeDtypeStruct((rows, D), jnp.bfloat16),
        in_specs=[vmem] * len(parts),
        out_specs=vmem,
        compiler_params=pltpu.CompilerParams(vmem_limit_bytes=8 * MIB),
        cost_estimate=pl.CostEstimate(flops=0, bytes_accessed=4 * rows * D, transcendentals=0),
        name="stack",
    )(*parts)


def combine_kernel(code_ref, attn_ref, r0, r1, r2, r3, out_ref):
    rows_at = lax.broadcasted_iota(jnp.int32, (ROWS, TOK), 0)
    code = code_ref[...]
    for q in range(4):
        c = slice(q * QUARTER, (q + 1) * QUARTER)
        total = attn_ref[:, c].astype(jnp.float32)
        for i, r in enumerate((r0, r1, r2, r3)):
            pick = (rows_at == code - i * ROWS + q * CAP).astype(jnp.bfloat16)
            total += lax.dot_general(pick, r[...], (((0,), (0,)), ((), ())), preferred_element_type=jnp.float32)
        out_ref[:, c] = total.astype(jnp.bfloat16)


def combine(code, attn, rows):
    vmem = pl.BlockSpec(memory_space=pltpu.VMEM)
    return pl.pallas_call(
        combine_kernel,
        out_shape=jax.ShapeDtypeStruct((TOK, D), jnp.bfloat16),
        in_specs=[vmem] * 6,
        out_specs=vmem,
        compiler_params=pltpu.CompilerParams(vmem_limit_bytes=14 * MIB),
        cost_estimate=pl.CostEstimate(flops=60_000_000, bytes_accessed=3_000_000, transcendentals=0),
        name="combine",
    )(code, attn, *rows)


def same_row(i, q):
    whole = lax.broadcasted_iota(jnp.int32, (ROWS, ROWS), 0) - i * CAP
    quarter = lax.broadcasted_iota(jnp.int32, (ROWS, ROWS), 1) - q * CAP
    return ((whole == quarter) & (whole >= 0) & (whole < CAP)).astype(jnp.bfloat16)


def unpack_kernel(p0, p1, p2, p3, out_ref):
    for q in range(4):
        total = None
        for i, p in enumerate((p0, p1, p2, p3)):
            term = jnp.dot(same_row(i, q), p[...], preferred_element_type=jnp.float32)
            total = term if total is None else total + term
        out_ref[:, q * QUARTER:(q + 1) * QUARTER] = total.astype(jnp.bfloat16)


def unpack(pieces):
    vmem = pl.BlockSpec(memory_space=pltpu.VMEM)
    return pl.pallas_call(
        unpack_kernel,
        out_shape=jax.ShapeDtypeStruct((ROWS, D), jnp.bfloat16),
        in_specs=[vmem] * 4,
        out_specs=vmem,
        compiler_params=pltpu.CompilerParams(vmem_limit_bytes=8 * MIB),
        cost_estimate=pl.CostEstimate(flops=2 * 4 * ROWS * ROWS * D, bytes_accessed=4 * ROWS * D, transcendentals=0),
        name="unpack",
    )(*pieces)


def add_and_pack_kernel(a, b, c, d, *outs):
    totals = [None] * 4
    for q in range(4):
        at = slice(q * QUARTER, (q + 1) * QUARTER)
        rows = sum(r[:, at].astype(jnp.float32) for r in (a, b, c, d)).astype(jnp.bfloat16)
        for i in range(4):
            term = lax.dot_general(same_row(i, q), rows, (((0,), (0,)), ((), ())), preferred_element_type=jnp.float32)
            totals[i] = term if totals[i] is None else totals[i] + term
    for o, total in zip(outs, totals):
        o[...] = total.astype(jnp.bfloat16)


def add_and_pack(parts):
    vmem = pl.BlockSpec(memory_space=pltpu.VMEM)
    return pl.pallas_call(
        add_and_pack_kernel,
        out_shape=tuple(jax.ShapeDtypeStruct((ROWS, QUARTER), jnp.bfloat16) for _ in range(4)),
        in_specs=[vmem] * 4,
        out_specs=(vmem,) * 4,
        compiler_params=pltpu.CompilerParams(vmem_limit_bytes=8 * MIB),
        cost_estimate=pl.CostEstimate(flops=2 * 4 * ROWS * ROWS * D, bytes_accessed=10 * ROWS * D, transcendentals=0),
        name="add_and_pack",
    )(*parts)


def add_up(parts):
    total = parts[0].astype(jnp.float32)
    for p in parts[1:]:
        total = total + p.astype(jnp.float32)
    return total.astype(jnp.bfloat16)


def after(value, *others):
    return lax.optimization_barrier((value, others))[0]


def per_device(queries, key_rows, value_rows, segments, swap_flags, expert_ids, norm_gain, gate_weight, up_weight, down_weight):
    dp = lax.axis_index("dp")
    z = lax.axis_index("expert") // 16
    info = jnp.stack([swap_flags[0], z // 2, 1 - 2 * (z % 2), dp]).astype(jnp.int32)

    across = device_pairs(lambda d, zz, y, x: (d, zz ^ 1, y, x))
    beside = device_pairs(lambda d, zz, y, x: (1 - d, zz, y, x))
    g_first = send(lax.dynamic_slice_in_dim(gate_weight, dp * HALF, CUT, 0), across)

    seg_local = segments.astype(jnp.bfloat16)
    q1, k1, v1, s1 = (send(a, beside) for a in (queries, key_rows, value_rows, seg_local))
    seg = jnp.where(swap_flags[0] > 0, s1, seg_local)[0].astype(jnp.float32)
    position = jnp.arange(TOK)
    allowed = (seg[:, None] == seg[None, :]) & (position[:, None] >= position[None, :])
    bias = jnp.where(allowed, jnp.float32(0), jnp.float32(-1e30))
    attn, code, *rows = attention(
        info, queries, q1, key_rows, k1, value_rows, v1, bias, expert_ids.reshape(1, TOK), norm_gain.reshape(1, D)
    )

    moved = [send(rows[k], to_expert(k)) for k in (1, 2, 3)]
    mine = unpack([rows[0]] + after(moved, g_first))
    g_rest = lax.dynamic_slice_in_dim(gate_weight, after(dp, k1) * HALF + CUT, HALF - CUT, 0)
    g_rest = send(after(g_rest, code), across)
    line = stack([mine] + [send(mine, plane_shift(1, s)) for s in (1, 3, 2)])
    c1, c3, c2 = (send(line, plane_shift(2, s)) for s in (1, 3, 2))
    u_half = lax.dynamic_slice_in_dim(up_weight, dp * HALF, HALF, 0)
    u_half = send(after(u_half, moved), across)

    own_gu = (gate_weight, up_weight)
    g_rest = hold(g_rest, 3 * HINT // 2)
    (h_line,) = hidden(info, [after(line, g_rest)], ("own",), own_gu)
    g_first, g_rest, u_half = after((g_first, g_rest, u_half), h_line)
    other_gu = (g_first, g_rest, send(g_first, beside), send(g_rest, beside), u_half, send(u_half, beside))
    (h_near,) = hidden(info, [c1, c3], ("own",), own_gu, HINT)
    wa = send(after(lax.dynamic_slice_in_dim(down_weight, dp * (FF // 2), FF // 2, 0), line), across)
    (h_other,) = hidden(info, [after(line, h_near), c1, c3], ("other",), other_gu)
    wa = hold(after(wa, (h_other, c2)), 3*HINT//2)
    own_last, other_last = hidden(info, [after(c2, wa)], ("own", "other"), own_gu + other_gu)

    wb = send(wa, beside)
    (far0,), (far1,) = down(info, [own_last], other_last, down_weight, wa, wb)
    outs0, outs1 = down(info, [h_line, h_near], h_other, down_weight, wa, after(wb, far0))

    relay0 = send(far0, plane_shift(2, 1))
    relay1 = send(far1, plane_shift(2, 3))
    plain0 = send(outs0[1], plane_shift(2, 3))
    plain1 = send(outs1[2], plane_shift(2, 1))
    both0 = send(add_up([outs0[2], relay0]), plane_shift(2, 1))
    both1 = send(add_up([outs1[1], relay1]), plane_shift(2, 3))
    halves = ((outs0[0], plain0, both0), (outs1[0], plain1, both1))
    back = line_sums(halves)
    pieces = add_and_pack([back[0]] + [send(b, plane_shift(1, s)) for b, s in zip(back[1:], (3, 1, 2))])
    returned = [pieces[0]] + [send(pieces[k], reverse(to_expert(k))) for k in (1, 2, 3)]
    return combine(code, attn, returned)


def solution(mesh):
    in_specs = (
        P(("dp", "expert"), None),
        P(("dp", "expert"), None),
        P(("dp", "expert"), None),
        P(("dp", "expert"), None),
        P("expert"),
        P(("dp", "expert"), None),
        P(),
        P(None, "expert"),
        P(None, "expert"),
        P("expert", None),
    )
    out_specs = P(("dp", "expert"), None)
    return jax.shard_map(
        per_device, mesh=mesh, in_specs=in_specs, out_specs=out_specs, check_vma=False
    )
```
